32 devices in a mesh: wide: 4 (over z), narrow: 8 (over y, x, core).
Axes of the slice: x: 2, y: 2, z: 4, core: 2. Of those that a mesh axis runs over, the one named last changes fastest.
Arguments:
- tokens: bfloat16 [4096, 2048], P(('wide', 'narrow')), may hold values from -6 to 6
- out_grad: bfloat16 [4096, 2048], P(('wide', 'narrow')), may hold values from -6 to 6
- expert_ids: int32 [4096, 6], P(('wide', 'narrow')), may hold values from 0 to 15, as said below
- gates: bfloat16 [4096, 6], P(('wide', 'narrow')), may hold values from 0.049804688 to 0.5
- w_gate: bfloat16 [32, 2048, 704], P(('wide', 'narrow')), may hold values from -0.125 to 0.125
- w_up: bfloat16 [32, 2048, 704], P(('wide', 'narrow')), may hold values from -0.125 to 0.125
- w_down: bfloat16 [32, 704, 2048], P(('wide', 'narrow')), may hold values from -0.15625 to 0.15625
- gate_saved: bfloat16 [32, 1536, 704], P(('wide', 'narrow')), may hold values from -6 to 6
- up_saved: bfloat16 [32, 1536, 704], P(('wide', 'narrow')), may hold values from -6 to 6
Outputs:
- token_grad: bfloat16 [4096, 2048], P(('wide', 'narrow'))
- grad_gate: bfloat16 [32, 2048, 704], P(('wide', 'narrow'))
- grad_up: bfloat16 [32, 2048, 704], P(('wide', 'narrow'))
- grad_down: bfloat16 [32, 704, 2048], P(('wide', 'narrow'))
The draws below stay inside these ranges and needn't reach their ends.
Inputs may be any that keep to these rules, and one draw needn't show every extreme that they name: `expert_ids`: each row names 6 different experts, 2 in each of exactly 3 of the groups of 4 consecutive experts; for every device and every group, exactly 96 of the device's tokens name experts of that group.
All inputs are finite; a program needn't handle non-finite values.
Results may differ from the reference program's by a relative error of at most 0.012.
Values may be sent and summed in bfloat16 or wider, within the bound.
A program may use at most 192 MiB of HBM per device.

```python
import math
import jax
import jax.numpy as jnp
from jax import lax

D = 2048
FF = 1408
TOP = 6
TOK_DEV = 128
NODES_MAX = 3
EXPERTS = 16
EXPERTS_NODE = 4
PER_NODE = 2
CAP = 48
HALF = 704
SLICES = 32
TOKENS = 4096
N_WIDE = 4
N_NARROW = 8


def draw_expert_ids(key, part):
    key = jax.random.fold_in(key, 11)
    key_offset, key_spots, key_level, key_noise = jax.random.split(key, 4)
    groups = EXPERTS // EXPERTS_NODE
    holders = TOKENS // TOK_DEV
    offset_score = jax.random.randint(key_offset, (holders, groups), 0, 4096) * groups + jnp.arange(groups, dtype=jnp.int32)[None, :]
    unused, offsets = lax.top_k(offset_score, NODES_MAX)
    spot_keys = jax.random.split(key_spots, holders)
    spots = jax.vmap(lambda k: jax.random.permutation(k, TOK_DEV))(spot_keys).astype(jnp.int32)
    base = spots % groups
    nodes = (base[:, :, None] + offsets[:, None, :].astype(jnp.int32)) % groups
    nodes = nodes.reshape(TOKENS, NODES_MAX)
    level = jax.random.randint(key_level, (EXPERTS,), 0, 4) * 1024
    noise = jax.random.randint(key_noise, (TOKENS, NODES_MAX, EXPERTS_NODE), 0, 2048)
    local_range = jnp.arange(EXPERTS_NODE, dtype=jnp.int32)
    expert_of = nodes[:, :, None] * EXPERTS_NODE + local_range[None, None, :]
    score = (level[expert_of] + noise) * EXPERTS_NODE + local_range[None, None, :]
    unused_two, local = lax.top_k(score, PER_NODE)
    picked = nodes[:, :, None] * EXPERTS_NODE + local.astype(jnp.int32)
    return picked.reshape(TOKENS, TOP).astype(jnp.int32)


def block_levels(rng, dims, cuts, least, largest):
    factor_of = 1.0
    for position, blocks in cuts:
        heights = jax.random.uniform(jax.random.fold_in(jax.random.fold_in(rng, 6), position), (blocks,), jnp.float32, least / len(cuts), largest / len(cuts))
        factor_of = factor_of * jnp.repeat(jnp.exp(heights), dims[position] // blocks).reshape((-1,) + (1,) * (len(dims) - 1 - position))
    return factor_of


def bell_draw(key, extent, deviation, most, cuts=(), kind=jnp.bfloat16):
    loudness = block_levels(key, extent, cuts, -0.22, 0.18) if cuts else 1.0
    drawn = jax.random.normal(key, extent, jnp.float32) * deviation * loudness
    return jnp.minimum(jnp.maximum(drawn, -most), most).astype(kind)


def setup_inputs(seed: int = 0) -> dict:
    key_list = jax.random.split(jax.random.key(seed), 10)
    tokens = bell_draw(key_list[0], (TOKENS, D), 1.0, 6.0, ((0, 32),))
    out_grad = bell_draw(key_list[1], (TOKENS, D), 1.0, 6.0, ((0, 32),))
    expert_ids = draw_expert_ids(jax.random.fold_in(key_list[9], 71), 0)
    gates = jnp.clip(jnp.exp(math.log(0.5) - 2.306499 * jax.random.uniform(key_list[3], (TOKENS, TOP), jnp.float32) ** block_levels(key_list[3], (TOKENS, TOP), ((0, 32),), -0.2, 0.2)), 0.049804688, 0.5).astype(jnp.bfloat16)
    w_gate = bell_draw(key_list[4], (SLICES, D, HALF), D ** -0.5, 0.125, ((0, 32),))
    w_up = bell_draw(key_list[5], (SLICES, D, HALF), D ** -0.5, 0.125, ((0, 32),))
    w_down = bell_draw(key_list[6], (SLICES, HALF, D), FF ** -0.5, 0.15625, ((0, 32),))
    gate_saved = bell_draw(key_list[7], (SLICES, N_WIDE * N_NARROW * CAP, HALF), 1.0, 6.0, ((0, 32),))
    up_saved = bell_draw(key_list[8], (SLICES, N_WIDE * N_NARROW * CAP, HALF), 1.0, 6.0, ((0, 32),))
    return dict(tokens=tokens, out_grad=out_grad, expert_ids=expert_ids, gates=gates, w_gate=w_gate, w_up=w_up, w_down=w_down, gate_saved=gate_saved, up_saved=up_saved)


def slot_tables(ids, gate_rows, experts, slot_cap):
    count = ids.shape[0]
    flat = ids.reshape(-1)
    picked = (flat[:, None] == jnp.arange(experts, dtype=jnp.int32)[None, :]).astype(jnp.int32)
    before = jnp.cumsum(picked, axis=0) - picked
    rank = jnp.sum(before * picked, axis=1)
    keep = rank < slot_cap
    place = flat * slot_cap + rank
    hits = (jnp.arange(experts * slot_cap, dtype=jnp.int32)[:, None] == place[None, :]) & keep[None, :]
    hits = hits.reshape(experts * slot_cap, count, ids.shape[1])
    placed = jnp.any(hits, axis=2).astype(jnp.float32)
    weighted = jnp.sum(jnp.where(hits, gate_rows[None, :, :], jnp.float32(0.0)), axis=2)
    return placed, weighted


def reference(tokens, out_grad, expert_ids, gates, w_gate, w_up, w_down, gate_saved, up_saved):
    devices = N_WIDE * N_NARROW
    experts = devices // 2
    high = lax.Precision.HIGHEST
    ids3 = expert_ids.reshape(devices, TOK_DEV, TOP)
    gates3 = gates.astype(jnp.float32).reshape(devices, TOK_DEV, TOP)
    placed, weighted = jax.vmap(lambda i, g: slot_tables(i, g, experts, CAP))(ids3, gates3)
    x32 = tokens.reshape(devices, TOK_DEV, D).astype(jnp.float32)
    dy32 = out_grad.reshape(devices, TOK_DEV, D).astype(jnp.float32)
    full_gate = w_gate.reshape(experts, 2, D, HALF).transpose(0, 2, 1, 3).reshape(experts, D, FF)
    full_up = w_up.reshape(experts, 2, D, HALF).transpose(0, 2, 1, 3).reshape(experts, D, FF)
    full_down = w_down.reshape(experts, FF, D)
    stored_gate = gate_saved.reshape(experts, 2, devices * CAP, HALF).transpose(0, 2, 1, 3).reshape(experts, devices * CAP, FF)
    stored_up = up_saved.reshape(experts, 2, devices * CAP, HALF).transpose(0, 2, 1, 3).reshape(experts, devices * CAP, FF)

    def one_expert(carry, expert):
        start = (expert * CAP).astype(jnp.int32)
        pick = lax.dynamic_slice_in_dim(placed, start, CAP, 1)
        scaled = lax.dynamic_slice_in_dim(weighted, start, CAP, 1)
        rows_x = jnp.einsum("sct,std->scd", pick, x32, precision=high).astype(jnp.bfloat16).reshape(-1, D)
        rows_dy = jnp.einsum("sct,std->scd", scaled, dy32, precision=high).astype(jnp.bfloat16).reshape(-1, D)
        wg = lax.dynamic_index_in_dim(full_gate, expert, 0, keepdims=False)
        wu = lax.dynamic_index_in_dim(full_up, expert, 0, keepdims=False)
        wd = lax.dynamic_index_in_dim(full_down, expert, 0, keepdims=False)
        gate_pre = lax.dynamic_index_in_dim(stored_gate, expert, 0, keepdims=False).astype(jnp.float32)
        up_pre = lax.dynamic_index_in_dim(stored_up, expert, 0, keepdims=False).astype(jnp.float32)
        sigma = jax.nn.sigmoid(gate_pre)
        silu = gate_pre * sigma
        act = (silu * up_pre).astype(jnp.bfloat16)
        act_grad = jnp.dot(rows_dy, wd.T, preferred_element_type=jnp.float32)
        up_grad = (act_grad * silu).astype(jnp.bfloat16)
        gate_grad = (act_grad * up_pre * sigma * (1.0 + gate_pre * (1.0 - sigma))).astype(jnp.bfloat16)
        slot_grad = jnp.dot(gate_grad, wg.T, preferred_element_type=jnp.float32) + jnp.dot(up_grad, wu.T, preferred_element_type=jnp.float32)
        back = jnp.einsum("sct,scd->std", pick, slot_grad.reshape(devices, CAP, D), precision=high)
        grad_one = jnp.dot(rows_x.T, gate_grad, preferred_element_type=jnp.float32).astype(jnp.bfloat16)
        grad_two = jnp.dot(rows_x.T, up_grad, preferred_element_type=jnp.float32).astype(jnp.bfloat16)
        grad_three = jnp.dot(act.T, rows_dy, preferred_element_type=jnp.float32).astype(jnp.bfloat16)
        return carry + back, (grad_one, grad_two, grad_three)

    start_carry = jnp.zeros((devices, TOK_DEV, D), jnp.float32)
    total, grads = lax.scan(one_expert, start_carry, jnp.arange(experts, dtype=jnp.int32))
    token_grad = total.reshape(devices * TOK_DEV, D).astype(jnp.bfloat16)
    grad_gate = grads[0].reshape(experts, D, 2, HALF).transpose(0, 2, 1, 3).reshape(devices, D, HALF)
    grad_up = grads[1].reshape(experts, D, 2, HALF).transpose(0, 2, 1, 3).reshape(devices, D, HALF)
    grad_down = grads[2].reshape(devices, HALF, D)
    return (token_grad, grad_gate, grad_up, grad_down)
```

```python
import jax
import jax.numpy as jnp
from jax import lax
from jax.sharding import PartitionSpec as P

BF = jnp.bfloat16
F32 = jnp.float32
ACROSS = (((0,), (0,)), ((), ()))
INNER = (((1,), (1,)), ((), ()))


def swap(value, axis, shift):
    if shift == 0:
        return value
    size = lax.axis_size(axis)
    return lax.ppermute(value, axis, [(i, i ^ shift) for i in range(size)])


def route_tables(ids, gates, experts, cap):
    count = ids.shape[0]
    hit = ids[:, :, None] == jnp.arange(experts, dtype=jnp.int32)[None, None, :]
    picked = jnp.any(hit, axis=1)
    gate = jnp.sum(jnp.where(hit, gates.astype(F32)[:, :, None], 0.0), axis=1)
    row = lax.broadcasted_iota(jnp.int32, (count, count), 0)
    col = lax.broadcasted_iota(jnp.int32, (count, count), 1)
    rank = jnp.dot((col < row).astype(BF), picked.astype(BF), preferred_element_type=F32)
    rank = jnp.where(picked & (rank < cap), rank, -1.0)
    return picked, rank, gate


def local(tokens, out_grad, expert_ids, gates, w_gate, w_up, w_down, gate_saved, up_saved):
    n_wide = lax.axis_size("wide")
    n_narrow = lax.axis_size("narrow")
    devices = n_wide * n_narrow
    experts = devices // 2
    spots = n_narrow // 2
    count, width = tokens.shape
    half = w_gate.shape[2]
    cap = gate_saved.shape[1] // devices
    rows = count * (expert_ids.shape[1] // 2) // n_wide
    my_wide = lax.axis_index("wide")
    my_narrow = lax.axis_index("narrow")
    my_spot = my_narrow // 2
    me = my_wide * n_narrow + my_narrow

    picked, rank, gate = route_tables(expert_ids, gates, experts, cap)
    groups = my_wide ^ jnp.arange(n_wide, dtype=jnp.int32)
    member = jnp.any(picked.reshape(count, n_wide, spots), axis=2)
    row = lax.broadcasted_iota(jnp.int32, (count, count), 0)
    col = lax.broadcasted_iota(jnp.int32, (count, count), 1)
    place = jnp.dot((col < row).astype(BF), member.astype(BF), preferred_element_type=F32)
    place = jnp.where(member, place, -1.0)
    place = jnp.take(place, groups, axis=1)
    pack = (place[:, :, None] == jnp.arange(rows, dtype=F32)[None, None, :]).astype(BF)
    pack = pack.reshape(count, n_wide * rows)
    info = jnp.concatenate([rank.reshape(count, n_wide, spots), gate.reshape(count, n_wide, spots)], 2)
    info = jnp.take(info, groups, axis=1).astype(BF)

    order = me ^ jnp.arange(devices, dtype=jnp.int32)
    gate_rows = jnp.take(gate_saved[0].reshape(devices, cap, half), order, axis=0)
    up_rows = jnp.take(up_saved[0].reshape(devices, cap, half), order, axis=0)
    gate_rows = gate_rows.reshape(n_wide, n_narrow * cap, half)
    up_rows = up_rows.reshape(n_wide, n_narrow * cap, half)

    spot_order = my_spot ^ jnp.arange(spots, dtype=jnp.int32)
    weight_gate, weight_up, weight_down = w_gate[0], w_up[0], w_down[0]

    arrived = []
    for step in range(n_wide):
        mine = pack[:, step * rows : (step + 1) * rows]
        sent_x = lax.dot_general(mine, tokens, ACROSS, preferred_element_type=F32).astype(BF)
        sent_dy = lax.dot_general(mine, out_grad, ACROSS, preferred_element_type=F32).astype(BF)
        sent_info = lax.dot_general(mine, info[:, step], ACROSS, preferred_element_type=F32).astype(BF)
        sent_info = jnp.pad(sent_info, ((0, 0), (0, 128 - 2 * spots)))
        sent = jnp.concatenate([sent_x, sent_dy, sent_info], axis=1)
        arrived.append(swap(sent, "wide", step))

    tables, all_x, all_dy, all_act, all_gate, all_up, partials = [], [], [], [], [], [], []
    for step in range(n_wide):
        got = arrived[step]
        got_rank = jnp.take(got[:, 2 * width : 2 * width + spots], spot_order, axis=1).astype(F32)
        got_gate = jnp.take(got[:, 2 * width + spots : 2 * width + 2 * spots], spot_order, axis=1)
        hits = got_rank[:, :, None] == jnp.arange(cap, dtype=F32)[None, None, :]
        table = hits.astype(BF).reshape(rows, spots * cap)
        scaled = jnp.where(hits, got_gate[:, :, None], jnp.zeros((), BF)).reshape(rows, spots * cap)
        tables.append(table)
        x_slot = lax.dot_general(table, got[:, :width], ACROSS, preferred_element_type=F32).astype(BF)
        dy_slot = lax.dot_general(
            scaled, got[:, width : 2 * width], ACROSS, preferred_element_type=F32
        ).astype(BF)
        both = jnp.stack([x_slot.reshape(spots, cap, width), dy_slot.reshape(spots, cap, width)], 1)
        plane = jnp.stack([swap(both[k], "narrow", 2 * k) for k in range(spots)])
        chip = jnp.stack([plane, swap(plane, "narrow", 1)], 1)
        rows_x = chip[:, :, 0].reshape(n_narrow * cap, width)
        rows_dy = chip[:, :, 1].reshape(n_narrow * cap, width)
        gate_pre = gate_rows[step].astype(F32)
        up_pre = up_rows[step].astype(F32)
        sigma = jax.nn.sigmoid(gate_pre)
        silu = gate_pre * sigma
        act = (silu * up_pre).astype(BF)
        act_grad = lax.dot_general(rows_dy, weight_down, INNER, preferred_element_type=F32)
        up_grad = (act_grad * silu).astype(BF)
        gate_grad = (act_grad * up_pre * sigma * (1.0 + gate_pre * (1.0 - sigma))).astype(BF)
        partial = lax.dot_general(gate_grad, weight_gate, INNER, preferred_element_type=F32)
        partial = partial + lax.dot_general(up_grad, weight_up, INNER, preferred_element_type=F32)
        all_x.append(rows_x)
        all_dy.append(rows_dy)
        all_act.append(act)
        all_gate.append(gate_grad)
        all_up.append(up_grad)
        partials.append(partial.astype(BF).reshape(spots, 2, cap, width))

    token_grad = jnp.zeros((count, width), F32)
    for step in range(n_wide):
        partial = partials[step]
        whole = partial[:, 0].astype(F32) + swap(partial[:, 1], "narrow", 1).astype(F32)
        whole = whole.astype(BF)
        back = jnp.concatenate([swap(whole[k], "narrow", 2 * k) for k in range(spots)], 0)
        part = jnp.dot(tables[step], back, preferred_element_type=F32).astype(BF)
        part = swap(part, "wide", step)
        token_grad = token_grad + jnp.dot(
            pack[:, step * rows : (step + 1) * rows], part, preferred_element_type=F32
        )

    cat_x = jnp.concatenate(all_x, 0)
    cat_dy = jnp.concatenate(all_dy, 0)
    cat_act = jnp.concatenate(all_act, 0)
    cat_gate = jnp.concatenate(all_gate, 0)
    cat_up = jnp.concatenate(all_up, 0)
    grad_gate = lax.dot_general(cat_x, cat_gate, ACROSS, preferred_element_type=F32).astype(BF)
    grad_up = lax.dot_general(cat_x, cat_up, ACROSS, preferred_element_type=F32).astype(BF)
    grad_down = lax.dot_general(cat_act, cat_dy, ACROSS, preferred_element_type=F32).astype(BF)
    return (token_grad.astype(BF), grad_gate[None], grad_up[None], grad_down[None])


def solution(mesh):
    row = P(("wide", "narrow"), None)
    slab = P(("wide", "narrow"), None, None)
    return jax.shard_map(
        local,
        mesh=mesh,
        in_specs=(row, row, row, row, slab, slab, slab, slab, slab),
        out_specs=(row, slab, slab, slab),
        check_vma=False,
    )
```

```python
import functools

import jax
import jax.numpy as jnp
from jax import lax
from jax.experimental import pallas as pl
from jax.experimental.pallas import tpu as pltpu
from jax.sharding import PartitionSpec as P

BF = jnp.bfloat16
F32 = jnp.float32
ACROSS = (((0,), (0,)), ((), ()))
INNER = (((1,), (1,)), ((), ()))
MESH = pl.DeviceIdType.MESH
VMEM_BYTES = 61 * 1024 * 1024


def swap(value, axis, shift):
    if shift == 0:
        return value
    size = lax.axis_size(axis)
    return lax.ppermute(value, axis, [(i, i ^ shift) for i in range(size)])


def route_tables(ids, gates, experts, cap):
    count = ids.shape[0]
    hit = ids[:, :, None] == jnp.arange(experts, dtype=jnp.int32)[None, None, :]
    picked = jnp.any(hit, axis=1)
    gate = jnp.sum(jnp.where(hit, gates.astype(F32)[:, :, None], 0.0), axis=1)
    row = lax.broadcasted_iota(jnp.int32, (count, count), 0)
    col = lax.broadcasted_iota(jnp.int32, (count, count), 1)
    rank = jnp.dot((col < row).astype(BF), picked.astype(BF), preferred_element_type=F32)
    rank = jnp.where(picked & (rank < cap), rank, -1.0)
    return picked, rank, gate


def local_permutes(tokens, out_grad, expert_ids, gates, w_gate, w_up, w_down, gate_saved, up_saved):
    n_wide = lax.axis_size("wide")
    n_narrow = lax.axis_size("narrow")
    devices = n_wide * n_narrow
    experts = devices // 2
    spots = n_narrow // 2
    count, width = tokens.shape
    half = w_gate.shape[2]
    cap = gate_saved.shape[1] // devices
    rows = count * (expert_ids.shape[1] // 2) // n_wide
    my_wide = lax.axis_index("wide")
    my_narrow = lax.axis_index("narrow")
    my_spot = my_narrow // 2
    me = my_wide * n_narrow + my_narrow

    picked, rank, gate = route_tables(expert_ids, gates, experts, cap)
    groups = my_wide ^ jnp.arange(n_wide, dtype=jnp.int32)
    member = jnp.any(picked.reshape(count, n_wide, spots), axis=2)
    row = lax.broadcasted_iota(jnp.int32, (count, count), 0)
    col = lax.broadcasted_iota(jnp.int32, (count, count), 1)
    place = jnp.dot((col < row).astype(BF), member.astype(BF), preferred_element_type=F32)
    place = jnp.where(member, place, -1.0)
    place = jnp.take(place, groups, axis=1)
    pack = (place[:, :, None] == jnp.arange(rows, dtype=F32)[None, None, :]).astype(BF)
    pack = pack.reshape(count, n_wide * rows)
    info = jnp.concatenate([rank.reshape(count, n_wide, spots), gate.reshape(count, n_wide, spots)], 2)
    info = jnp.take(info, groups, axis=1).astype(BF)

    order = me ^ jnp.arange(devices, dtype=jnp.int32)
    gate_rows = jnp.take(gate_saved[0].reshape(devices, cap, half), order, axis=0)
    up_rows = jnp.take(up_saved[0].reshape(devices, cap, half), order, axis=0)
    gate_rows = gate_rows.reshape(n_wide, n_narrow * cap, half)
    up_rows = up_rows.reshape(n_wide, n_narrow * cap, half)

    spot_order = my_spot ^ jnp.arange(spots, dtype=jnp.int32)
    weight_gate, weight_up, weight_down = w_gate[0], w_up[0], w_down[0]

    arrived = []
    for step in range(n_wide):
        mine = pack[:, step * rows : (step + 1) * rows]
        sent_x = lax.dot_general(mine, tokens, ACROSS, preferred_element_type=F32).astype(BF)
        sent_dy = lax.dot_general(mine, out_grad, ACROSS, preferred_element_type=F32).astype(BF)
        sent_info = lax.dot_general(mine, info[:, step], ACROSS, preferred_element_type=F32).astype(BF)
        sent_info = jnp.pad(sent_info, ((0, 0), (0, 128 - 2 * spots)))
        sent = jnp.concatenate([sent_x, sent_dy, sent_info], axis=1)
        arrived.append(swap(sent, "wide", step))

    tables, all_x, all_dy, all_act, all_gate, all_up, partials = [], [], [], [], [], [], []
    for step in range(n_wide):
        got = arrived[step]
        got_rank = jnp.take(got[:, 2 * width : 2 * width + spots], spot_order, axis=1).astype(F32)
        got_gate = jnp.take(got[:, 2 * width + spots : 2 * width + 2 * spots], spot_order, axis=1)
        hits = got_rank[:, :, None] == jnp.arange(cap, dtype=F32)[None, None, :]
        table = hits.astype(BF).reshape(rows, spots * cap)
        scaled = jnp.where(hits, got_gate[:, :, None], jnp.zeros((), BF)).reshape(rows, spots * cap)
        tables.append(table)
        x_slot = lax.dot_general(table, got[:, :width], ACROSS, preferred_element_type=F32).astype(BF)
        dy_slot = lax.dot_general(
            scaled, got[:, width : 2 * width], ACROSS, preferred_element_type=F32
        ).astype(BF)
        both = jnp.stack([x_slot.reshape(spots, cap, width), dy_slot.reshape(spots, cap, width)], 1)
        plane = jnp.stack([swap(both[k], "narrow", 2 * k) for k in range(spots)])
        chip = jnp.stack([plane, swap(plane, "narrow", 1)], 1)
        rows_x = chip[:, :, 0].reshape(n_narrow * cap, width)
        rows_dy = chip[:, :, 1].reshape(n_narrow * cap, width)
        gate_pre = gate_rows[step].astype(F32)
        up_pre = up_rows[step].astype(F32)
        sigma = jax.nn.sigmoid(gate_pre)
        silu = gate_pre * sigma
        act = (silu * up_pre).astype(BF)
        act_grad = lax.dot_general(rows_dy, weight_down, INNER, preferred_element_type=F32)
        up_grad = (act_grad * silu).astype(BF)
        gate_grad = (act_grad * up_pre * sigma * (1.0 + gate_pre * (1.0 - sigma))).astype(BF)
        partial = lax.dot_general(gate_grad, weight_gate, INNER, preferred_element_type=F32)
        partial = partial + lax.dot_general(up_grad, weight_up, INNER, preferred_element_type=F32)
        all_x.append(rows_x)
        all_dy.append(rows_dy)
        all_act.append(act)
        all_gate.append(gate_grad)
        all_up.append(up_grad)
        partials.append(partial.astype(BF).reshape(spots, 2, cap, width))

    token_grad = jnp.zeros((count, width), F32)
    for step in range(n_wide):
        partial = partials[step]
        whole = partial[:, 0].astype(F32) + swap(partial[:, 1], "narrow", 1).astype(F32)
        whole = whole.astype(BF)
        back = jnp.concatenate([swap(whole[k], "narrow", 2 * k) for k in range(spots)], 0)
        part = jnp.dot(tables[step], back, preferred_element_type=F32).astype(BF)
        part = swap(part, "wide", step)
        token_grad = token_grad + jnp.dot(
            pack[:, step * rows : (step + 1) * rows], part, preferred_element_type=F32
        )

    cat_x = jnp.concatenate(all_x, 0)
    cat_dy = jnp.concatenate(all_dy, 0)
    cat_act = jnp.concatenate(all_act, 0)
    cat_gate = jnp.concatenate(all_gate, 0)
    cat_up = jnp.concatenate(all_up, 0)
    grad_gate = lax.dot_general(cat_x, cat_gate, ACROSS, preferred_element_type=F32).astype(BF)
    grad_up = lax.dot_general(cat_x, cat_up, ACROSS, preferred_element_type=F32).astype(BF)
    grad_down = lax.dot_general(cat_act, cat_dy, ACROSS, preferred_element_type=F32).astype(BF)
    return (token_grad.astype(BF), grad_gate[None], grad_up[None], grad_down[None])


def exchange_kernel(
    n_wide, n_narrow, cap, tokens_ref, grad_ref, pack_ref, spread_ref, info_ref, wg_hbm, wu_hbm,
    wd_hbm, gate_hbm, up_hbm, out_ref, x_hbm, dy_hbm, gg_hbm, ug_hbm, send, zbuf, stage_x, stage_dy,
    dy_rows, w_gate, w_up, w_down, gate_in, up_in, gg, ug, part, half_in, back, pick_out, pick_in,
    load_sem, keep_sem, save_sem, z_sem, px_sem, pd_sem, sx_sem, sd_sem, half_sem, back_sem, zb_sem,
):
    spots = n_narrow // 2
    width = tokens_ref.shape[1]
    rows = pack_ref.shape[1]
    slots = spots * cap
    chunk = n_narrow * cap
    mz = lax.axis_index("wide")
    mn = lax.axis_index("narrow")
    ms = mn // 2
    core = mn - 2 * ms
    sibling = ms * 2 + (1 - core)

    def plane_id(q):
        return (ms ^ q) * 2 + core

    def remote(src, dst, sems, wide, narrow):
        copy = pltpu.make_async_remote_copy(
            src_ref=src, dst_ref=dst, send_sem=sems[0], recv_sem=sems[1],
            device_id=(wide, narrow), device_id_type=MESH,
        )
        copy.start()
        return copy

    def pair(sem, *index):
        return sem.at[(0, *index)], sem.at[(1, *index)]

    def here(src, dst, sem):
        copy = pltpu.make_async_copy(src, dst, sem)
        copy.start()
        return copy

    loads = [
        here(wd_hbm.at[0], w_down, load_sem.at[0]),
        here(wg_hbm.at[0], w_gate, load_sem.at[1]),
        here(wu_hbm.at[0], w_up, load_sem.at[2]),
    ]
    saved = []
    for k in range(n_wide):
        source = pl.ds((mz ^ k) * chunk, chunk)
        saved.append((
            here(gate_hbm.at[0, source], gate_in.at[k], load_sem.at[3 + 2 * k]),
            here(up_hbm.at[0, source], up_in.at[k], load_sem.at[4 + 2 * k]),
        ))

    barrier = pltpu.get_barrier_semaphore()
    for k in range(1, n_wide):
        pl.semaphore_signal(barrier, inc=1, device_id=(mz ^ k, mn), device_id_type=MESH)
    for q in range(1, spots):
        pl.semaphore_signal(barrier, inc=1, device_id=(mz, plane_id(q)), device_id_type=MESH)
    pl.semaphore_signal(barrier, inc=1, device_id=(mz, sibling), device_id_type=MESH)

    def pack(k):
        send[k, :, :width] = jnp.dot(
            pack_ref[k], tokens_ref[...], preferred_element_type=F32
        ).astype(BF)
        send[k, :, width : 2 * width] = jnp.dot(
            pack_ref[k], grad_ref[...], preferred_element_type=F32
        ).astype(BF)
        send[k, :, 2 * width :] = info_ref[k]

    z_copies = [None] * n_wide
    for k in list(range(1, n_wide)) + [0]:
        pack(k)
        if k == 1:
            pl.semaphore_wait(barrier, n_wide - 1 + spots - 1 + 1)
        if k:
            z_copies[k] = remote(send.at[k], zbuf.at[k], pair(z_sem, k), mz ^ k, mn)

    ended, kept = [], []
    plane, shared = {}, {}

    def make_slots(k):
        if k:
            z_copies[k].wait_recv()
        got = zbuf if k else send
        info = jnp.transpose(got[k, :, 2 * width :].astype(F32))
        line = lax.broadcasted_iota(jnp.int32, (slots, rows), 0)
        rank = jnp.zeros((slots, rows), F32)
        gate = jnp.zeros((slots, rows), F32)
        rest = line
        for e in range(spots):
            inside = (line >= e * cap) & (line < (e + 1) * cap)
            rank = jnp.where(inside, info[e : e + 1, :], rank)
            gate = jnp.where(inside, info[spots + e : spots + e + 1, :], gate)
            rest = jnp.where(inside, line - e * cap, rest)
        hit = rank == rest.astype(F32)
        table = jnp.where(hit, 1.0, 0.0).astype(BF)
        scaled = jnp.where(hit, gate, 0.0).astype(BF)
        stage_dy[k] = jnp.dot(
            scaled, got[k, :, width : 2 * width], preferred_element_type=F32
        ).astype(BF).reshape(spots, cap, width)
        for q in range(1, spots):
            to = (mz ^ k) * n_narrow + mn
            plane[k, q, 1] = remote(
                stage_dy.at[k, ms ^ q], dy_rows.at[to], pair(pd_sem, k, q), mz, plane_id(q)
            )
        stage_x[k] = jnp.dot(
            table, got[k, :, :width], preferred_element_type=F32
        ).astype(BF).reshape(spots, cap, width)
        for q in range(1, spots):
            to = (mz ^ k) * n_narrow + mn
            plane[k, q, 0] = remote(
                stage_x.at[k, ms ^ q], x_hbm.at[to], pair(px_sem, k, q), mz, plane_id(q)
            )
        to = (mz ^ k) * n_narrow + mn
        kept.append((
            here(stage_dy.at[k, ms], dy_rows.at[to], keep_sem.at[k, 0]),
            here(stage_x.at[k, ms], x_hbm.at[to], keep_sem.at[k, 1]),
        ))
        shared[k, 0, 1] = remote(
            stage_dy.at[k, ms], dy_rows.at[to], pair(sd_sem, k, 0), mz, sibling
        )
        shared[k, 0, 0] = remote(stage_x.at[k, ms], x_hbm.at[to], pair(sx_sem, k, 0), mz, sibling)

    def share(k):
        for which, rows_ref, sem in ((1, dy_rows, sd_sem), (0, x_hbm, sx_sem)):
            for q in range(1, spots):
                plane[k, q, which].wait_recv()
                at = (mz ^ k) * n_narrow + plane_id(q)
                shared[k, q, which] = remote(
                    rows_ref.at[at], rows_ref.at[at], pair(sem, k, q), mz, sibling
                )

    halves = [None] * n_wide
    saves = []

    def expert(k):
        kept[k][0].wait()
        for q in range(spots):
            shared[k, q, 1].wait_recv()
        if k == 0:
            loads[0].wait()
        for copy in saved[k]:
            copy.wait()
        source = pl.ds((mz ^ k) * n_narrow, n_narrow)
        dy = dy_rows[source].reshape(chunk, width)
        act_grad = lax.dot_general(dy, w_down[...], INNER, preferred_element_type=F32)
        gate_pre = gate_in[k].astype(F32)
        up_pre = up_in[k].astype(F32)
        sigma = jax.nn.sigmoid(gate_pre)
        ug[k] = (act_grad * (gate_pre * sigma)).astype(BF)
        gg[k] = (act_grad * up_pre * sigma * (1.0 + gate_pre * (1.0 - sigma))).astype(BF)
        source_rows = pl.ds((mz ^ k) * chunk, chunk)
        saves.append(here(gg.at[k], gg_hbm.at[source_rows], save_sem.at[k, 0]))
        saves.append(here(ug.at[k], ug_hbm.at[source_rows], save_sem.at[k, 1]))
        saves.append(here(dy_rows.at[source], dy_hbm.at[source], save_sem.at[k, 2]))
        if k == 0:
            loads[1].wait()
            loads[2].wait()
        tile = 512

        def columns(j, carry):
            at = pl.ds(pl.multiple_of(j * tile, tile), tile)
            value = lax.dot_general(gg[k], w_gate[at, :], INNER, preferred_element_type=F32)
            value = value + lax.dot_general(ug[k], w_up[at, :], INNER, preferred_element_type=F32)
            value = value.astype(BF).reshape(spots, 2, cap, tile)
            for c in range(2):
                part[k, c, :, :, at] = value[:, c]
            return carry

        lax.fori_loop(0, width // tile, columns, 0)
        halves[k] = remote(part.at[k, 1 - core], half_in.at[k], pair(half_sem, k), mz, sibling)

    returned = {}

    def give_back(k):
        halves[k].wait_recv()
        whole = part[k, core].astype(F32) + half_in[k].astype(F32)
        part[k, core] = whole.astype(BF)
        for q in range(1, spots):
            returned[k, q] = remote(
                part.at[k, core, ms ^ q], back.at[k, ms], pair(back_sem, k, q), mz, plane_id(q)
            )
        returned[k, 0] = here(part.at[k, core, ms], back.at[k, ms], keep_sem.at[k, 2])

    z_back = [None] * n_wide

    def pick(k):
        for q in range(1, spots):
            returned[k, q].wait_recv()
        returned[k, 0].wait()
        got = zbuf if k else send
        info = got[k, :, 2 * width :].astype(F32)
        line = lax.broadcasted_iota(jnp.int32, (rows, slots), 1)
        rank = jnp.zeros((rows, slots), F32)
        rest = line
        for e in range(spots):
            inside = (line >= e * cap) & (line < (e + 1) * cap)
            rank = jnp.where(inside, info[:, e : e + 1], rank)
            rest = jnp.where(inside, line - e * cap, rest)
        table = jnp.where(rank == rest.astype(F32), 1.0, 0.0).astype(BF)
        value = jnp.dot(table, back[k].reshape(slots, width), preferred_element_type=F32)
        pick_out[k] = value.astype(BF)
        if k:
            z_back[k] = remote(pick_out.at[k], pick_in.at[k], pair(zb_sem, k), mz ^ k, mn)

    last = n_wide - 1
    for k in range(n_wide + 4):
        if k <= last:
            make_slots(k)
        if 1 <= k <= last + 1:
            expert(k - 1)
        if 3 <= k <= last + 3:
            pick(k - 3)
        if k <= last:
            share(k)
        if 2 <= k <= last + 2:
            give_back(k - 2)

    total = jnp.dot(spread_ref[0], pick_out[0], preferred_element_type=F32)
    for k in range(1, n_wide):
        z_back[k].wait_recv()
        total = total + jnp.dot(spread_ref[k], pick_in[k], preferred_element_type=F32)
    out_ref[...] = total.astype(BF)

    for k in range(n_wide):
        kept[k][1].wait()
        for q in range(spots):
            shared[k, q, 0].wait_recv()
            shared[k, q, 0].wait_send()
            shared[k, q, 1].wait_send()
            if q:
                plane[k, q, 0].wait_send()
                plane[k, q, 1].wait_send()
                returned[k, q].wait_send()
        halves[k].wait_send()
        if k:
            z_copies[k].wait_send()
            z_back[k].wait_send()
    for copy in saves:
        copy.wait()


def exchange(tokens, out_grad, pack, spread, info, w_gate, w_up, w_down, gate_saved, up_saved):
    n_wide, n_narrow = lax.axis_size("wide"), lax.axis_size("narrow")
    devices = n_wide * n_narrow
    spots = n_narrow // 2
    count, width = tokens.shape
    rows = pack.shape[1]
    half = w_gate.shape[2]
    cap = gate_saved.shape[1] // devices
    chunk = n_narrow * cap
    wide_row = 2 * width + info.shape[2]
    flops = 6 * devices * cap * width * half
    vmem = pl.BlockSpec(memory_space=pltpu.VMEM)
    hbm = pl.BlockSpec(memory_space=pl.ANY)
    sem = pltpu.SemaphoreType.DMA
    return pl.pallas_call(
        functools.partial(exchange_kernel, n_wide, n_narrow, cap),
        out_shape=(
            jax.ShapeDtypeStruct((count, width), BF),
            jax.ShapeDtypeStruct((devices, cap, width), BF),
            jax.ShapeDtypeStruct((devices, cap, width), BF),
            jax.ShapeDtypeStruct((devices * cap, half), BF),
            jax.ShapeDtypeStruct((devices * cap, half), BF),
        ),
        in_specs=[vmem] * 5 + [hbm] * 5,
        out_specs=(vmem, hbm, hbm, hbm, hbm),
        scratch_shapes=[
            pltpu.VMEM((n_wide, rows, wide_row), BF),
            pltpu.VMEM((n_wide, rows, wide_row), BF),
            pltpu.VMEM((n_wide, spots, cap, width), BF),
            pltpu.VMEM((n_wide, spots, cap, width), BF),
            pltpu.VMEM((devices, cap, width), BF),
            pltpu.VMEM((width, half), BF),
            pltpu.VMEM((width, half), BF),
            pltpu.VMEM((half, width), BF),
            pltpu.VMEM((n_wide, chunk, half), BF),
            pltpu.VMEM((n_wide, chunk, half), BF),
            pltpu.VMEM((n_wide, chunk, half), BF),
            pltpu.VMEM((n_wide, chunk, half), BF),
            pltpu.VMEM((n_wide, 2, spots, cap, width), BF),
            pltpu.VMEM((n_wide, spots, cap, width), BF),
            pltpu.VMEM((n_wide, spots, cap, width), BF),
            pltpu.VMEM((n_wide, rows, width), BF),
            pltpu.VMEM((n_wide, rows, width), BF),
            sem((3 + 2 * n_wide,)),
            sem((n_wide, 3)),
            sem((n_wide, 3)),
            sem((2, n_wide)),
            sem((2, n_wide, spots)),
            sem((2, n_wide, spots)),
            sem((2, n_wide, spots)),
            sem((2, n_wide, spots)),
            sem((2, n_wide)),
            sem((2, n_wide, spots)),
            sem((2, n_wide)),
        ],
        compiler_params=pltpu.CompilerParams(
            collective_id=0, has_side_effects=True, vmem_limit_bytes=VMEM_BYTES
        ),
        cost_estimate=pl.CostEstimate(flops=flops, bytes_accessed=40_000_000, transcendentals=0),
    )(tokens, out_grad, pack, spread, info, w_gate, w_up, w_down, gate_saved, up_saved)


def local_kernel(tokens, out_grad, expert_ids, gates, w_gate, w_up, w_down, gate_saved, up_saved):
    n_wide = lax.axis_size("wide")
    n_narrow = lax.axis_size("narrow")
    devices = n_wide * n_narrow
    experts = devices // 2
    spots = n_narrow // 2
    count, width = tokens.shape
    cap = gate_saved.shape[1] // devices
    rows = count * (expert_ids.shape[1] // 2) // n_wide
    picked, rank, gate = route_tables(expert_ids, gates, experts, cap)
    groups = lax.axis_index("wide") ^ jnp.arange(n_wide, dtype=jnp.int32)
    member = jnp.any(picked.reshape(count, n_wide, spots), axis=2)
    row = lax.broadcasted_iota(jnp.int32, (count, count), 0)
    col = lax.broadcasted_iota(jnp.int32, (count, count), 1)
    place = jnp.dot((col < row).astype(BF), member.astype(BF), preferred_element_type=F32)
    place = jnp.take(jnp.where(member, place, -1.0), groups, axis=1).T
    number = jnp.arange(rows, dtype=F32)
    spread = (place[:, :, None] == number[None, None, :]).astype(BF)
    pack = (place[:, None, :] == number[None, :, None]).astype(BF)
    info = jnp.concatenate([rank.reshape(count, n_wide, spots), gate.reshape(count, n_wide, spots)], 2)
    info = jnp.take(info, groups, axis=1).astype(BF).transpose(1, 0, 2)
    info = jnp.pad(info, ((0, 0), (0, 0), (0, 128 - 2 * spots)))
    info = jnp.einsum("krt,ktc->krc", pack, info, preferred_element_type=F32).astype(BF)
    token_grad, rows_x, rows_dy, gate_grad, up_grad = exchange(
        tokens, out_grad, pack, spread, info, w_gate, w_up, w_down, gate_saved, up_saved
    )
    rows_x = rows_x.reshape(devices * cap, width)
    rows_dy = rows_dy.reshape(devices * cap, width)
    act = (jax.nn.silu(gate_saved[0].astype(F32)) * up_saved[0].astype(F32)).astype(BF)
    grad_gate = lax.dot_general(rows_x, gate_grad, ACROSS, preferred_element_type=F32).astype(BF)
    grad_up = lax.dot_general(rows_x, up_grad, ACROSS, preferred_element_type=F32).astype(BF)
    grad_down = lax.dot_general(act, rows_dy, ACROSS, preferred_element_type=F32).astype(BF)
    return (token_grad, grad_gate[None], grad_up[None], grad_down[None])


def local(tokens, out_grad, expert_ids, gates, w_gate, w_up, w_down, gate_saved, up_saved):
    slots = gate_saved.shape[1]
    cap = slots // (lax.axis_size("wide") * lax.axis_size("narrow"))
    fits = 8 * slots * tokens.shape[1] <= VMEM_BYTES and cap % 16 == 0
    body = local_kernel if fits else local_permutes
    return body(tokens, out_grad, expert_ids, gates, w_gate, w_up, w_down, gate_saved, up_saved)


def solution(mesh):
    row = P(("wide", "narrow"), None)
    slab = P(("wide", "narrow"), None, None)
    return jax.shard_map(
        local,
        mesh=mesh,
        in_specs=(row, row, row, row, slab, slab, slab, slab, slab),
        out_specs=(row, slab, slab, slab),
        check_vma=False,
    )
```

```python
import functools

import jax
import jax.numpy as jnp
from jax import lax
from jax.experimental import pallas as pl
from jax.experimental.pallas import tpu as pltpu
from jax.sharding import PartitionSpec as P

BF = jnp.bfloat16
F32 = jnp.float32
ACROSS = (((0,), (0,)), ((), ()))
INNER = (((1,), (1,)), ((), ()))
MESH = pl.DeviceIdType.MESH
VMEM_BYTES = 61 * 1024 * 1024


def swap(value, axis, shift):
    if shift == 0:
        return value
    size = lax.axis_size(axis)
    return lax.ppermute(value, axis, [(i, i ^ shift) for i in range(size)])


def route_tables(ids, gates, experts, cap):
    count = ids.shape[0]
    hit = ids[:, :, None] == jnp.arange(experts, dtype=jnp.int32)[None, None, :]
    picked = jnp.any(hit, axis=1)
    gate = jnp.sum(jnp.where(hit, gates.astype(F32)[:, :, None], 0.0), axis=1)
    row = lax.broadcasted_iota(jnp.int32, (count, count), 0)
    col = lax.broadcasted_iota(jnp.int32, (count, count), 1)
    rank = jnp.dot((col < row).astype(BF), picked.astype(BF), preferred_element_type=F32)
    rank = jnp.where(picked & (rank < cap), rank, -1.0)
    return picked, rank, gate


def local_permutes(tokens, out_grad, expert_ids, gates, w_gate, w_up, w_down, gate_saved, up_saved):
    n_wide = lax.axis_size("wide")
    n_narrow = lax.axis_size("narrow")
    devices = n_wide * n_narrow
    experts = devices // 2
    spots = n_narrow // 2
    count, width = tokens.shape
    half = w_gate.shape[2]
    cap = gate_saved.shape[1] // devices
    rows = count * (expert_ids.shape[1] // 2) // n_wide
    my_wide = lax.axis_index("wide")
    my_narrow = lax.axis_index("narrow")
    my_spot = my_narrow // 2
    me = my_wide * n_narrow + my_narrow

    picked, rank, gate = route_tables(expert_ids, gates, experts, cap)
    groups = my_wide ^ jnp.arange(n_wide, dtype=jnp.int32)
    member = jnp.any(picked.reshape(count, n_wide, spots), axis=2)
    row = lax.broadcasted_iota(jnp.int32, (count, count), 0)
    col = lax.broadcasted_iota(jnp.int32, (count, count), 1)
    place = jnp.dot((col < row).astype(BF), member.astype(BF), preferred_element_type=F32)
    place = jnp.where(member, place, -1.0)
    place = jnp.take(place, groups, axis=1)
    pack = (place[:, :, None] == jnp.arange(rows, dtype=F32)[None, None, :]).astype(BF)
    pack = pack.reshape(count, n_wide * rows)
    info = jnp.concatenate([rank.reshape(count, n_wide, spots), gate.reshape(count, n_wide, spots)], 2)
    info = jnp.take(info, groups, axis=1).astype(BF)

    order = me ^ jnp.arange(devices, dtype=jnp.int32)
    gate_rows = jnp.take(gate_saved[0].reshape(devices, cap, half), order, axis=0)
    up_rows = jnp.take(up_saved[0].reshape(devices, cap, half), order, axis=0)
    gate_rows = gate_rows.reshape(n_wide, n_narrow * cap, half)
    up_rows = up_rows.reshape(n_wide, n_narrow * cap, half)

    spot_order = my_spot ^ jnp.arange(spots, dtype=jnp.int32)
    weight_gate, weight_up, weight_down = w_gate[0], w_up[0], w_down[0]

    arrived = []
    for step in range(n_wide):
        mine = pack[:, step * rows : (step + 1) * rows]
        sent_x = lax.dot_general(mine, tokens, ACROSS, preferred_element_type=F32).astype(BF)
        sent_dy = lax.dot_general(mine, out_grad, ACROSS, preferred_element_type=F32).astype(BF)
        sent_info = lax.dot_general(mine, info[:, step], ACROSS, preferred_element_type=F32).astype(BF)
        sent_info = jnp.pad(sent_info, ((0, 0), (0, 128 - 2 * spots)))
        sent = jnp.concatenate([sent_x, sent_dy, sent_info], axis=1)
        arrived.append(swap(sent, "wide", step))

    tables, all_x, all_dy, all_act, all_gate, all_up, partials = [], [], [], [], [], [], []
    for step in range(n_wide):
        got = arrived[step]
        got_rank = jnp.take(got[:, 2 * width : 2 * width + spots], spot_order, axis=1).astype(F32)
        got_gate = jnp.take(got[:, 2 * width + spots : 2 * width + 2 * spots], spot_order, axis=1)
        hits = got_rank[:, :, None] == jnp.arange(cap, dtype=F32)[None, None, :]
        table = hits.astype(BF).reshape(rows, spots * cap)
        scaled = jnp.where(hits, got_gate[:, :, None], jnp.zeros((), BF)).reshape(rows, spots * cap)
        tables.append(table)
        x_slot = lax.dot_general(table, got[:, :width], ACROSS, preferred_element_type=F32).astype(BF)
        dy_slot = lax.dot_general(
            scaled, got[:, width : 2 * width], ACROSS, preferred_element_type=F32
        ).astype(BF)
        both = jnp.stack([x_slot.reshape(spots, cap, width), dy_slot.reshape(spots, cap, width)], 1)
        plane = jnp.stack([swap(both[k], "narrow", 2 * k) for k in range(spots)])
        chip = jnp.stack([plane, swap(plane, "narrow", 1)], 1)
        rows_x = chip[:, :, 0].reshape(n_narrow * cap, width)
        rows_dy = chip[:, :, 1].reshape(n_narrow * cap, width)
        gate_pre = gate_rows[step].astype(F32)
        up_pre = up_rows[step].astype(F32)
        sigma = jax.nn.sigmoid(gate_pre)
        silu = gate_pre * sigma
        act = (silu * up_pre).astype(BF)
        act_grad = lax.dot_general(rows_dy, weight_down, INNER, preferred_element_type=F32)
        up_grad = (act_grad * silu).astype(BF)
        gate_grad = (act_grad * up_pre * sigma * (1.0 + gate_pre * (1.0 - sigma))).astype(BF)
        partial = lax.dot_general(gate_grad, weight_gate, INNER, preferred_element_type=F32)
        partial = partial + lax.dot_general(up_grad, weight_up, INNER, preferred_element_type=F32)
        all_x.append(rows_x)
        all_dy.append(rows_dy)
        all_act.append(act)
        all_gate.append(gate_grad)
        all_up.append(up_grad)
        partials.append(partial.astype(BF).reshape(spots, 2, cap, width))

    token_grad = jnp.zeros((count, width), F32)
    for step in range(n_wide):
        partial = partials[step]
        whole = partial[:, 0].astype(F32) + swap(partial[:, 1], "narrow", 1).astype(F32)
        whole = whole.astype(BF)
        back = jnp.concatenate([swap(whole[k], "narrow", 2 * k) for k in range(spots)], 0)
        part = jnp.dot(tables[step], back, preferred_element_type=F32).astype(BF)
        part = swap(part, "wide", step)
        token_grad = token_grad + jnp.dot(
            pack[:, step * rows : (step + 1) * rows], part, preferred_element_type=F32
        )

    cat_x = jnp.concatenate(all_x, 0)
    cat_dy = jnp.concatenate(all_dy, 0)
    cat_act = jnp.concatenate(all_act, 0)
    cat_gate = jnp.concatenate(all_gate, 0)
    cat_up = jnp.concatenate(all_up, 0)
    grad_gate = lax.dot_general(cat_x, cat_gate, ACROSS, preferred_element_type=F32).astype(BF)
    grad_up = lax.dot_general(cat_x, cat_up, ACROSS, preferred_element_type=F32).astype(BF)
    grad_down = lax.dot_general(cat_act, cat_dy, ACROSS, preferred_element_type=F32).astype(BF)
    return (token_grad.astype(BF), grad_gate[None], grad_up[None], grad_down[None])


def exchange_kernel(
    n_wide, n_narrow, cap, tokens_ref, grad_ref, pack_ref, spread_ref, info_ref, wg_hbm, wu_hbm,
    wd_hbm, gate_hbm, up_hbm, out_ref, x_hbm, dy_hbm, gg_hbm, ug_hbm, send_x, send_dy, zx, zdy,
    stage_x, stage_dy, dy_rows, w_gate, w_up, w_down, gate_in, up_in, gg, ug, gg_rows, ug_rows, part, half_in, back, pick_out, pick_in,
    load_sem, keep_sem, save_sem, zx_sem, zdy_sem, px_sem, pd_sem, sx_sem, sd_sem, half_sem, back_sem, zb_sem,
):
    spots = n_narrow // 2
    width = tokens_ref.shape[1]
    rows = pack_ref.shape[1]
    slots = spots * cap
    chunk = n_narrow * cap
    mz = lax.axis_index("wide")
    mn = lax.axis_index("narrow")
    ms = mn // 2
    core = mn - 2 * ms
    sibling = ms * 2 + (1 - core)

    def plane_id(q):
        return (ms ^ q) * 2 + core

    def remote(src, dst, sems, wide, narrow):
        copy = pltpu.make_async_remote_copy(
            src_ref=src, dst_ref=dst, send_sem=sems[0], recv_sem=sems[1],
            device_id=(wide, narrow), device_id_type=MESH,
        )
        copy.start()
        return copy

    def pair(sem, *index):
        return sem.at[(0, *index)], sem.at[(1, *index)]

    def here(src, dst, sem):
        copy = pltpu.make_async_copy(src, dst, sem)
        copy.start()
        return copy

    loads = [
        here(wd_hbm.at[0], w_down, load_sem.at[0]),
        here(wg_hbm.at[0], w_gate, load_sem.at[1]),
        here(wu_hbm.at[0], w_up, load_sem.at[2]),
    ]
    saved = []
    for k in range(n_wide):
        source = pl.ds(pl.multiple_of((mz ^ k) * chunk, 128), chunk)
        saved.append((
            here(gate_hbm.at[0, :, source], gate_in.at[k], load_sem.at[3 + 2 * k]),
            here(up_hbm.at[0, :, source], up_in.at[k], load_sem.at[4 + 2 * k]),
        ))

    barrier = pltpu.get_barrier_semaphore()
    for k in range(1, n_wide):
        pl.semaphore_signal(barrier, inc=1, device_id=(mz ^ k, mn), device_id_type=MESH)
    for q in range(1, spots):
        pl.semaphore_signal(barrier, inc=1, device_id=(mz, plane_id(q)), device_id_type=MESH)
    pl.semaphore_signal(barrier, inc=1, device_id=(mz, sibling), device_id_type=MESH)

    def pack_dy(k):
        send_dy[k, :, :width] = jnp.dot(
            pack_ref[k], grad_ref[...], preferred_element_type=F32
        ).astype(BF)
        send_dy[k, :, width:] = info_ref[k]

    def pack_x(k):
        send_x[k] = jnp.dot(pack_ref[k], tokens_ref[...], preferred_element_type=F32).astype(BF)

    z_dy, z_x = [None] * n_wide, [None] * n_wide

    def start_dy(k):
        z_dy[k] = remote(send_dy.at[k], zdy.at[k], pair(zdy_sem, k), mz ^ k, mn)

    def start_x(k):
        z_x[k] = remote(send_x.at[k], zx.at[k], pair(zx_sem, k), mz ^ k, mn)

    pack_dy(2)
    pl.semaphore_wait(barrier, n_wide - 1 + spots - 1 + 1)
    start_dy(2)
    pack_dy(1)
    start_dy(1)
    pack_dy(0)

    kept_dy, kept_x = {}, {}
    plane, shared = {}, {}

    def tables(k):
        got = zdy if k else send_dy
        info = jnp.transpose(got[k, :, width:].astype(F32))
        line = lax.broadcasted_iota(jnp.int32, (slots, rows), 0)
        rank = jnp.zeros((slots, rows), F32)
        gate = jnp.zeros((slots, rows), F32)
        rest = line
        for e in range(spots):
            inside = (line >= e * cap) & (line < (e + 1) * cap)
            rank = jnp.where(inside, info[e : e + 1, :], rank)
            gate = jnp.where(inside, info[spots + e : spots + e + 1, :], gate)
            rest = jnp.where(inside, line - e * cap, rest)
        return rank == rest.astype(F32), gate

    def slots_dy(k):
        if k:
            z_dy[k].wait_recv()
        got = zdy if k else send_dy
        hit, gate = tables(k)
        scaled = jnp.where(hit, gate, 0.0).astype(BF)
        stage_dy[k] = jnp.dot(scaled, got[k, :, :width], preferred_element_type=F32).astype(
            BF
        ).reshape(spots, cap, width)
        to = (mz ^ k) * n_narrow + mn
        for q in range(1, spots):
            plane[k, q, 1] = remote(
                stage_dy.at[k, ms ^ q], dy_rows.at[to], pair(pd_sem, k, q), mz, plane_id(q)
            )
        kept_dy[k] = here(stage_dy.at[k, ms], dy_rows.at[to], keep_sem.at[k, 0])
        shared[k, 0, 1] = remote(
            stage_dy.at[k, ms], dy_rows.at[to], pair(sd_sem, k, 0), mz, sibling
        )

    def slots_x(k):
        if k:
            z_x[k].wait_recv()
        got = zx if k else send_x
        table = jnp.where(tables(k)[0], 1.0, 0.0).astype(BF)
        stage_x[k] = jnp.dot(table, got[k], preferred_element_type=F32).astype(BF).reshape(
            spots, cap, width
        )
        to = (mz ^ k) * n_narrow + mn
        for q in range(1, spots):
            plane[k, q, 0] = remote(
                stage_x.at[k, ms ^ q], x_hbm.at[to], pair(px_sem, k, q), mz, plane_id(q)
            )
        kept_x[k] = here(stage_x.at[k, ms], x_hbm.at[to], keep_sem.at[k, 1])
        shared[k, 0, 0] = remote(stage_x.at[k, ms], x_hbm.at[to], pair(sx_sem, k, 0), mz, sibling)

    def share(k, which, rows_ref, sem):
        for q in range(1, spots):
            plane[k, q, which].wait_recv()
            at = (mz ^ k) * n_narrow + plane_id(q)
            shared[k, q, which] = remote(
                rows_ref.at[at], rows_ref.at[at], pair(sem, k, q), mz, sibling
            )

    halves = [None] * n_wide
    saves = []

    def expert(k):
        kept_dy[k].wait()
        for q in range(spots):
            shared[k, q, 1].wait_recv()
        if k == 0:
            loads[0].wait()
        for copy in saved[k]:
            copy.wait()
        source = pl.ds((mz ^ k) * n_narrow, n_narrow)
        dy = dy_rows[source].reshape(chunk, width)
        act_grad = lax.dot_general(w_down[...], dy, INNER, preferred_element_type=F32)
        gate_pre = gate_in[k].astype(F32)
        up_pre = up_in[k].astype(F32)
        sigma = jax.nn.sigmoid(gate_pre)
        up_grad = act_grad * (gate_pre * sigma)
        gate_grad = act_grad * up_pre * sigma * (1.0 + gate_pre * (1.0 - sigma))
        ug[k] = up_grad.astype(BF)
        gg[k] = gate_grad.astype(BF)
        ug_rows[...] = jnp.transpose(ug[k])
        gg_rows[...] = jnp.transpose(gg[k])
        source_rows = pl.ds(pl.multiple_of((mz ^ k) * chunk, 128), chunk)
        saves.append(here(gg.at[k], gg_hbm.at[:, source_rows], save_sem.at[k, 0]))
        saves.append(here(ug.at[k], ug_hbm.at[:, source_rows], save_sem.at[k, 1]))
        saves.append(here(dy_rows.at[source], dy_hbm.at[source], save_sem.at[k, 2]))
        if k == 0:
            loads[1].wait()
            loads[2].wait()
        tile = 512

        def columns(j, carry):
            at = pl.ds(pl.multiple_of(j * tile, tile), tile)
            value = jnp.dot(gg_rows[...], w_gate[:, at], preferred_element_type=F32)
            value = value + jnp.dot(ug_rows[...], w_up[:, at], preferred_element_type=F32)
            value = value.astype(BF).reshape(spots, 2, cap, tile)
            for c in range(2):
                part[k, c, :, :, at] = value[:, c]
            return carry

        lax.fori_loop(0, width // tile, columns, 0)
        halves[k] = remote(part.at[k, 1 - core], half_in.at[k], pair(half_sem, k), mz, sibling)

    returned = {}

    def give_back(k):
        halves[k].wait_recv()
        whole = part[k, core].astype(F32) + half_in[k].astype(F32)
        part[k, core] = whole.astype(BF)
        for q in range(1, spots):
            returned[k, q] = remote(
                part.at[k, core, ms ^ q], back.at[k, ms], pair(back_sem, k, q), mz, plane_id(q)
            )
        returned[k, 0] = here(part.at[k, core, ms], back.at[k, ms], keep_sem.at[k, 2])

    z_back = [None] * n_wide

    def pick(k):
        for q in range(1, spots):
            returned[k, q].wait_recv()
        returned[k, 0].wait()
        got = zdy if k else send_dy
        info = got[k, :, width:].astype(F32)
        line = lax.broadcasted_iota(jnp.int32, (rows, slots), 1)
        rank = jnp.zeros((rows, slots), F32)
        rest = line
        for e in range(spots):
            inside = (line >= e * cap) & (line < (e + 1) * cap)
            rank = jnp.where(inside, info[:, e : e + 1], rank)
            rest = jnp.where(inside, line - e * cap, rest)
        table = jnp.where(rank == rest.astype(F32), 1.0, 0.0).astype(BF)
        value = jnp.dot(table, back[k].reshape(slots, width), preferred_element_type=F32)
        pick_out[k] = value.astype(BF)
        if k:
            z_back[k] = remote(pick_out.at[k], pick_in.at[k], pair(zb_sem, k), mz ^ k, mn)

    def share_dy(k):
        share(k, 1, dy_rows, sd_sem)

    def share_x(k):
        share(k, 0, x_hbm, sx_sem)

    slots_dy(0)
    pack_x(0)
    pack_x(1)
    pack_dy(3)
    share_dy(0)
    slots_x(0)
    slots_dy(1)
    z_dy[2].wait_send()
    start_dy(3)
    start_x(1)
    slots_dy(2)
    pack_x(2)
    pack_x(3)
    expert(0)
    share_dy(1)
    share_x(0)
    expert(1)
    share_dy(2)
    give_back(0)
    slots_dy(3)
    z_dy[3].wait_send()
    start_x(2)
    expert(2)
    give_back(1)
    slots_x(1)
    share_dy(3)
    pick(0)
    expert(3)
    give_back(2)
    z_x[2].wait_send()
    start_x(3)
    pick(1)
    slots_x(2)
    give_back(3)
    share_x(1)
    pick(2)
    share_x(2)
    slots_x(3)
    pick(3)
    share_x(3)

    total = jnp.dot(spread_ref[0], pick_out[0], preferred_element_type=F32)
    for k in range(1, n_wide):
        z_back[k].wait_recv()
        total = total + jnp.dot(spread_ref[k], pick_in[k], preferred_element_type=F32)
    out_ref[...] = total.astype(BF)

    for k in range(n_wide):
        kept_x[k].wait()
        for q in range(spots):
            shared[k, q, 0].wait_recv()
            shared[k, q, 0].wait_send()
            shared[k, q, 1].wait_send()
            if q:
                plane[k, q, 0].wait_send()
                plane[k, q, 1].wait_send()
                returned[k, q].wait_send()
        halves[k].wait_send()
        if k:
            if k == 1:
                z_dy[k].wait_send()
            if k != 2:
                z_x[k].wait_send()
            z_back[k].wait_send()
    for copy in saves:
        copy.wait()


def exchange(tokens, out_grad, pack, spread, info, w_gate, w_up, w_down, gate_saved, up_saved):
    n_wide, n_narrow = lax.axis_size("wide"), lax.axis_size("narrow")
    devices = n_wide * n_narrow
    spots = n_narrow // 2
    count, width = tokens.shape
    rows = pack.shape[1]
    half = w_gate.shape[1]
    cap = gate_saved.shape[2] // devices
    chunk = n_narrow * cap
    wide_row = width + info.shape[2]
    flops = 6 * devices * cap * width * half
    vmem = pl.BlockSpec(memory_space=pltpu.VMEM)
    hbm = pl.BlockSpec(memory_space=pl.ANY)
    sem = pltpu.SemaphoreType.DMA
    return pl.pallas_call(
        functools.partial(exchange_kernel, n_wide, n_narrow, cap),
        out_shape=(
            jax.ShapeDtypeStruct((count, width), BF),
            jax.ShapeDtypeStruct((devices, cap, width), BF),
            jax.ShapeDtypeStruct((devices, cap, width), BF),
            jax.ShapeDtypeStruct((half, devices * cap), BF),
            jax.ShapeDtypeStruct((half, devices * cap), BF),
        ),
        in_specs=[vmem] * 5 + [hbm] * 5,
        out_specs=(vmem, hbm, hbm, hbm, hbm),
        scratch_shapes=[
            pltpu.VMEM((n_wide, rows, width), BF),
            pltpu.VMEM((n_wide, rows, wide_row), BF),
            pltpu.VMEM((n_wide, rows, width), BF),
            pltpu.VMEM((n_wide, rows, wide_row), BF),
            pltpu.VMEM((n_wide, spots, cap, width), BF),
            pltpu.VMEM((n_wide, spots, cap, width), BF),
            pltpu.VMEM((devices, cap, width), BF),
            pltpu.VMEM((half, width), BF),
            pltpu.VMEM((half, width), BF),
            pltpu.VMEM((half, width), BF),
            pltpu.VMEM((n_wide, half, chunk), BF),
            pltpu.VMEM((n_wide, half, chunk), BF),
            pltpu.VMEM((n_wide, half, chunk), BF),
            pltpu.VMEM((n_wide, half, chunk), BF),
            pltpu.VMEM((chunk, half), BF),
            pltpu.VMEM((chunk, half), BF),
            pltpu.VMEM((n_wide, 2, spots, cap, width), BF),
            pltpu.VMEM((n_wide, spots, cap, width), BF),
            pltpu.VMEM((n_wide, spots, cap, width), BF),
            pltpu.VMEM((n_wide, rows, width), BF),
            pltpu.VMEM((n_wide, rows, width), BF),
            sem((3 + 2 * n_wide,)),
            sem((n_wide, 3)),
            sem((n_wide, 3)),
            sem((2, n_wide)),
            sem((2, n_wide)),
            sem((2, n_wide, spots)),
            sem((2, n_wide, spots)),
            sem((2, n_wide, spots)),
            sem((2, n_wide, spots)),
            sem((2, n_wide)),
            sem((2, n_wide, spots)),
            sem((2, n_wide)),
        ],
        compiler_params=pltpu.CompilerParams(
            collective_id=0, has_side_effects=True, vmem_limit_bytes=VMEM_BYTES
        ),
        cost_estimate=pl.CostEstimate(flops=flops, bytes_accessed=40_000_000, transcendentals=0),
    )(tokens, out_grad, pack, spread, info, w_gate, w_up, w_down, gate_saved, up_saved)


def local_kernel(tokens, out_grad, expert_ids, gates, w_gate, w_up, w_down, gate_saved, up_saved):
    n_wide = lax.axis_size("wide")
    n_narrow = lax.axis_size("narrow")
    devices = n_wide * n_narrow
    experts = devices // 2
    spots = n_narrow // 2
    count, width = tokens.shape
    cap = gate_saved.shape[1] // devices
    rows = count * (expert_ids.shape[1] // 2) // n_wide
    picked, rank, gate = route_tables(expert_ids, gates, experts, cap)
    groups = lax.axis_index("wide") ^ jnp.arange(n_wide, dtype=jnp.int32)
    member = jnp.any(picked.reshape(count, n_wide, spots), axis=2)
    row = lax.broadcasted_iota(jnp.int32, (count, count), 0)
    col = lax.broadcasted_iota(jnp.int32, (count, count), 1)
    place = jnp.dot((col < row).astype(BF), member.astype(BF), preferred_element_type=F32)
    place = jnp.take(jnp.where(member, place, -1.0), groups, axis=1).T
    number = jnp.arange(rows, dtype=F32)
    spread = (place[:, :, None] == number[None, None, :]).astype(BF)
    pack = (place[:, None, :] == number[None, :, None]).astype(BF)
    info = jnp.concatenate([rank.reshape(count, n_wide, spots), gate.reshape(count, n_wide, spots)], 2)
    info = jnp.take(info, groups, axis=1).astype(BF).transpose(1, 0, 2)
    info = jnp.pad(info, ((0, 0), (0, 0), (0, 128 - 2 * spots)))
    info = jnp.einsum("krt,ktc->krc", pack, info, preferred_element_type=F32).astype(BF)
    turned_gate, turned_up = gate_saved.swapaxes(1, 2), up_saved.swapaxes(1, 2)
    token_grad, rows_x, rows_dy, gate_grad, up_grad = exchange(
        tokens, out_grad, pack, spread, info, w_gate.swapaxes(1, 2), w_up.swapaxes(1, 2), w_down,
        turned_gate, turned_up,
    )
    rows_x = rows_x.reshape(devices * cap, width)
    rows_dy = rows_dy.reshape(devices * cap, width)
    act = (jax.nn.silu(turned_gate[0].astype(F32)) * turned_up[0].astype(F32)).astype(BF)
    grad_gate = jnp.dot(gate_grad, rows_x, preferred_element_type=F32).astype(BF)
    grad_up = jnp.dot(up_grad, rows_x, preferred_element_type=F32).astype(BF)
    grad_down = jnp.dot(act, rows_dy, preferred_element_type=F32).astype(BF)
    return (token_grad, grad_gate.T[None], grad_up.T[None], grad_down[None])


def local(tokens, out_grad, expert_ids, gates, w_gate, w_up, w_down, gate_saved, up_saved):
    slots = gate_saved.shape[1]
    cap = slots // (lax.axis_size("wide") * lax.axis_size("narrow"))
    fits = 8 * slots * tokens.shape[1] <= VMEM_BYTES and cap % 16 == 0
    fits = fits and lax.axis_size("wide") == 4
    body = local_kernel if fits else local_permutes
    return body(tokens, out_grad, expert_ids, gates, w_gate, w_up, w_down, gate_saved, up_saved)


def solution(mesh):
    row = P(("wide", "narrow"), None)
    slab = P(("wide", "narrow"), None, None)
    return jax.shard_map(
        local,
        mesh=mesh,
        in_specs=(row, row, row, row, slab, slab, slab, slab, slab),
        out_specs=(row, slab, slab, slab),
        check_vma=False,
    )
```

```python
import functools

import jax
import jax.numpy as jnp
from jax import lax
from jax.experimental import pallas as pl
from jax.experimental.pallas import tpu as pltpu
from jax.sharding import PartitionSpec as P

BF = jnp.bfloat16
F32 = jnp.float32
ACROSS = (((0,), (0,)), ((), ()))
INNER = (((1,), (1,)), ((), ()))
MESH = pl.DeviceIdType.MESH
VMEM_BYTES = 63 * 1024 * 1024


def swap(value, axis, shift):
    if shift == 0:
        return value
    size = lax.axis_size(axis)
    return lax.ppermute(value, axis, [(i, i ^ shift) for i in range(size)])


def route_tables(ids, gates, experts, cap):
    count = ids.shape[0]
    hit = ids[:, :, None] == jnp.arange(experts, dtype=jnp.int32)[None, None, :]
    picked = jnp.any(hit, axis=1)
    gate = jnp.sum(jnp.where(hit, gates.astype(F32)[:, :, None], 0.0), axis=1)
    row = lax.broadcasted_iota(jnp.int32, (count, count), 0)
    col = lax.broadcasted_iota(jnp.int32, (count, count), 1)
    rank = jnp.dot((col < row).astype(BF), picked.astype(BF), preferred_element_type=F32)
    rank = jnp.where(picked & (rank < cap), rank, -1.0)
    return picked, rank, gate


def local_permutes(tokens, out_grad, expert_ids, gates, w_gate, w_up, w_down, gate_saved, up_saved):
    n_wide = lax.axis_size("wide")
    n_narrow = lax.axis_size("narrow")
    devices = n_wide * n_narrow
    experts = devices // 2
    spots = n_narrow // 2
    count, width = tokens.shape
    half = w_gate.shape[2]
    cap = gate_saved.shape[1] // devices
    rows = count * (expert_ids.shape[1] // 2) // n_wide
    my_wide = lax.axis_index("wide")
    my_narrow = lax.axis_index("narrow")
    my_spot = my_narrow // 2
    me = my_wide * n_narrow + my_narrow

    picked, rank, gate = route_tables(expert_ids, gates, experts, cap)
    groups = my_wide ^ jnp.arange(n_wide, dtype=jnp.int32)
    member = jnp.any(picked.reshape(count, n_wide, spots), axis=2)
    row = lax.broadcasted_iota(jnp.int32, (count, count), 0)
    col = lax.broadcasted_iota(jnp.int32, (count, count), 1)
    place = jnp.dot((col < row).astype(BF), member.astype(BF), preferred_element_type=F32)
    place = jnp.where(member, place, -1.0)
    place = jnp.take(place, groups, axis=1)
    pack = (place[:, :, None] == jnp.arange(rows, dtype=F32)[None, None, :]).astype(BF)
    pack = pack.reshape(count, n_wide * rows)
    info = jnp.concatenate([rank.reshape(count, n_wide, spots), gate.reshape(count, n_wide, spots)], 2)
    info = jnp.take(info, groups, axis=1).astype(BF)

    order = me ^ jnp.arange(devices, dtype=jnp.int32)
    gate_rows = jnp.take(gate_saved[0].reshape(devices, cap, half), order, axis=0)
    up_rows = jnp.take(up_saved[0].reshape(devices, cap, half), order, axis=0)
    gate_rows = gate_rows.reshape(n_wide, n_narrow * cap, half)
    up_rows = up_rows.reshape(n_wide, n_narrow * cap, half)

    spot_order = my_spot ^ jnp.arange(spots, dtype=jnp.int32)
    weight_gate, weight_up, weight_down = w_gate[0], w_up[0], w_down[0]

    arrived = []
    for step in range(n_wide):
        mine = pack[:, step * rows : (step + 1) * rows]
        sent_x = lax.dot_general(mine, tokens, ACROSS, preferred_element_type=F32).astype(BF)
        sent_dy = lax.dot_general(mine, out_grad, ACROSS, preferred_element_type=F32).astype(BF)
        sent_info = lax.dot_general(mine, info[:, step], ACROSS, preferred_element_type=F32).astype(BF)
        sent_info = jnp.pad(sent_info, ((0, 0), (0, 128 - 2 * spots)))
        sent = jnp.concatenate([sent_x, sent_dy, sent_info], axis=1)
        arrived.append(swap(sent, "wide", step))

    tables, all_x, all_dy, all_act, all_gate, all_up, partials = [], [], [], [], [], [], []
    for step in range(n_wide):
        got = arrived[step]
        got_rank = jnp.take(got[:, 2 * width : 2 * width + spots], spot_order, axis=1).astype(F32)
        got_gate = jnp.take(got[:, 2 * width + spots : 2 * width + 2 * spots], spot_order, axis=1)
        hits = got_rank[:, :, None] == jnp.arange(cap, dtype=F32)[None, None, :]
        table = hits.astype(BF).reshape(rows, spots * cap)
        scaled = jnp.where(hits, got_gate[:, :, None], jnp.zeros((), BF)).reshape(rows, spots * cap)
        tables.append(table)
        x_slot = lax.dot_general(table, got[:, :width], ACROSS, preferred_element_type=F32).astype(BF)
        dy_slot = lax.dot_general(
            scaled, got[:, width : 2 * width], ACROSS, preferred_element_type=F32
        ).astype(BF)
        both = jnp.stack([x_slot.reshape(spots, cap, width), dy_slot.reshape(spots, cap, width)], 1)
        plane = jnp.stack([swap(both[k], "narrow", 2 * k) for k in range(spots)])
        chip = jnp.stack([plane, swap(plane, "narrow", 1)], 1)
        rows_x = chip[:, :, 0].reshape(n_narrow * cap, width)
        rows_dy = chip[:, :, 1].reshape(n_narrow * cap, width)
        gate_pre = gate_rows[step].astype(F32)
        up_pre = up_rows[step].astype(F32)
        sigma = jax.nn.sigmoid(gate_pre)
        silu = gate_pre * sigma
        act = (silu * up_pre).astype(BF)
        act_grad = lax.dot_general(rows_dy, weight_down, INNER, preferred_element_type=F32)
        up_grad = (act_grad * silu).astype(BF)
        gate_grad = (act_grad * up_pre * sigma * (1.0 + gate_pre * (1.0 - sigma))).astype(BF)
        partial = lax.dot_general(gate_grad, weight_gate, INNER, preferred_element_type=F32)
        partial = partial + lax.dot_general(up_grad, weight_up, INNER, preferred_element_type=F32)
        all_x.append(rows_x)
        all_dy.append(rows_dy)
        all_act.append(act)
        all_gate.append(gate_grad)
        all_up.append(up_grad)
        partials.append(partial.astype(BF).reshape(spots, 2, cap, width))

    token_grad = jnp.zeros((count, width), F32)
    for step in range(n_wide):
        partial = partials[step]
        whole = partial[:, 0].astype(F32) + swap(partial[:, 1], "narrow", 1).astype(F32)
        whole = whole.astype(BF)
        back = jnp.concatenate([swap(whole[k], "narrow", 2 * k) for k in range(spots)], 0)
        part = jnp.dot(tables[step], back, preferred_element_type=F32).astype(BF)
        part = swap(part, "wide", step)
        token_grad = token_grad + jnp.dot(
            pack[:, step * rows : (step + 1) * rows], part, preferred_element_type=F32
        )

    cat_x = jnp.concatenate(all_x, 0)
    cat_dy = jnp.concatenate(all_dy, 0)
    cat_act = jnp.concatenate(all_act, 0)
    cat_gate = jnp.concatenate(all_gate, 0)
    cat_up = jnp.concatenate(all_up, 0)
    grad_gate = lax.dot_general(cat_x, cat_gate, ACROSS, preferred_element_type=F32).astype(BF)
    grad_up = lax.dot_general(cat_x, cat_up, ACROSS, preferred_element_type=F32).astype(BF)
    grad_down = lax.dot_general(cat_act, cat_dy, ACROSS, preferred_element_type=F32).astype(BF)
    return (token_grad.astype(BF), grad_gate[None], grad_up[None], grad_down[None])


def exchange_kernel(
    n_wide, n_narrow, cap, tokens_ref, grad_ref, pack_ref, spread_ref, info_ref, wg_hbm, wu_hbm,
    wd_hbm, gate_hbm, up_hbm, out_ref, x_last, down_hbm, gate_part,
    up_part, gg_hbm, ug_hbm, x_rows, send_x, send_dy, zx, zdy,
    stage_x, stage_dy, dy_rows, w_gate, w_up, w_down, gate_in, up_in, gg, ug, gg_rows, ug_rows, part, half_in, back, pick_out, pick_in,
    load_sem, keep_sem, save_sem, zx_sem, zdy_sem, px_sem, pd_sem, sx_sem, sd_sem, half_sem, back_sem, zb_sem,
):
    spots = n_narrow // 2
    width = tokens_ref.shape[1]
    rows = pack_ref.shape[1]
    slots = spots * cap
    chunk = n_narrow * cap
    mz = lax.axis_index("wide")
    mn = lax.axis_index("narrow")
    ms = mn // 2
    core = mn - 2 * ms
    sibling = ms * 2 + (1 - core)

    def plane_id(q):
        return (ms ^ q) * 2 + core

    def remote(src, dst, sems, wide, narrow):
        copy = pltpu.make_async_remote_copy(
            src_ref=src, dst_ref=dst, send_sem=sems[0], recv_sem=sems[1],
            device_id=(wide, narrow), device_id_type=MESH,
        )
        copy.start()
        return copy

    def pair(sem, *index):
        return sem.at[(0, *index)], sem.at[(1, *index)]

    def here(src, dst, sem):
        copy = pltpu.make_async_copy(src, dst, sem)
        copy.start()
        return copy

    loads = [
        here(wd_hbm.at[0], w_down, load_sem.at[0]),
        here(wg_hbm.at[0], w_gate, load_sem.at[1]),
        here(wu_hbm.at[0], w_up, load_sem.at[2]),
    ]
    saved = []
    for k in range(n_wide):
        source = pl.ds(pl.multiple_of((mz ^ k) * chunk, 128), chunk)
        saved.append((
            here(gate_hbm.at[0, :, source], gate_in.at[k], load_sem.at[3 + 2 * k]),
            here(up_hbm.at[0, :, source], up_in.at[k], load_sem.at[4 + 2 * k]),
        ))

    barrier = pltpu.get_barrier_semaphore()
    for k in range(1, n_wide):
        pl.semaphore_signal(barrier, inc=1, device_id=(mz ^ k, mn), device_id_type=MESH)
    for q in range(1, spots):
        pl.semaphore_signal(barrier, inc=1, device_id=(mz, plane_id(q)), device_id_type=MESH)
    pl.semaphore_signal(barrier, inc=1, device_id=(mz, sibling), device_id_type=MESH)

    def pack_dy(k):
        send_dy[k, :, :width] = jnp.dot(
            pack_ref[k], grad_ref[...], preferred_element_type=F32
        ).astype(BF)
        send_dy[k, :, width:] = info_ref[k]

    def pack_x(k):
        send_x[k] = jnp.dot(pack_ref[k], tokens_ref[...], preferred_element_type=F32).astype(BF)

    z_dy, z_x = [None] * n_wide, [None] * n_wide

    def start_dy(k):
        z_dy[k] = remote(send_dy.at[k], zdy.at[k], pair(zdy_sem, k), mz ^ k, mn)

    def start_x(k):
        z_x[k] = remote(send_x.at[k], zx.at[k], pair(zx_sem, k), mz ^ k, mn)

    pack_dy(2)
    pl.semaphore_wait(barrier, n_wide - 1 + spots - 1 + 1)
    start_dy(2)
    pack_dy(1)
    start_dy(1)
    pack_dy(0)

    kept_dy, kept_x = {}, {}
    plane, shared = {}, {}

    def tables(k):
        got = zdy if k else send_dy
        info = jnp.transpose(got[k, :, width:].astype(F32))
        line = lax.broadcasted_iota(jnp.int32, (slots, rows), 0)
        rank = jnp.zeros((slots, rows), F32)
        gate = jnp.zeros((slots, rows), F32)
        rest = line
        for e in range(spots):
            inside = (line >= e * cap) & (line < (e + 1) * cap)
            rank = jnp.where(inside, info[e : e + 1, :], rank)
            gate = jnp.where(inside, info[spots + e : spots + e + 1, :], gate)
            rest = jnp.where(inside, line - e * cap, rest)
        return rank == rest.astype(F32), gate

    def slots_dy(k):
        if k:
            z_dy[k].wait_recv()
        got = zdy if k else send_dy
        hit, gate = tables(k)
        scaled = jnp.where(hit, gate, 0.0).astype(BF)
        stage_dy[k] = jnp.dot(scaled, got[k, :, :width], preferred_element_type=F32).astype(
            BF
        ).reshape(spots, cap, width)
        to = (mz ^ k) * n_narrow + mn
        for q in range(1, spots):
            plane[k, q, 1] = remote(
                stage_dy.at[k, ms ^ q], dy_rows.at[to], pair(pd_sem, k, q), mz, plane_id(q)
            )
        kept_dy[k] = here(stage_dy.at[k, ms], dy_rows.at[to], keep_sem.at[k, 0])
        shared[k, 0, 1] = remote(
            stage_dy.at[k, ms], dy_rows.at[to], pair(sd_sem, k, 0), mz, sibling
        )

    def x_at(k, n):
        return x_last.at[n] if k == n_wide - 1 else x_rows.at[k, n]

    def slots_x(k):
        if k:
            z_x[k].wait_recv()
        got = zx if k else send_x
        table = jnp.where(tables(k)[0], 1.0, 0.0).astype(BF)
        stage_x[k] = jnp.dot(table, got[k], preferred_element_type=F32).astype(BF).reshape(
            spots, cap, width
        )
        to = x_at(k, mn)
        for q in range(1, spots):
            plane[k, q, 0] = remote(
                stage_x.at[k, ms ^ q], to, pair(px_sem, k, q), mz, plane_id(q)
            )
        kept_x[k] = here(stage_x.at[k, ms], to, keep_sem.at[k, 1])
        shared[k, 0, 0] = remote(stage_x.at[k, ms], to, pair(sx_sem, k, 0), mz, sibling)

    def share(k, which, sem):
        for q in range(1, spots):
            plane[k, q, which].wait_recv()
            if which:
                at = dy_rows.at[(mz ^ k) * n_narrow + plane_id(q)]
            else:
                at = x_at(k, plane_id(q))
            shared[k, q, which] = remote(at, at, pair(sem, k, q), mz, sibling)

    halves = [None] * n_wide
    saves = []

    def expert(k):
        kept_dy[k].wait()
        for q in range(spots):
            shared[k, q, 1].wait_recv()
        if k == 0:
            loads[0].wait()
        for copy in saved[k]:
            copy.wait()
        source = pl.ds((mz ^ k) * n_narrow, n_narrow)
        dy = dy_rows[source].reshape(chunk, width)
        act_grad = lax.dot_general(w_down[...], dy, INNER, preferred_element_type=F32)
        gate_pre = gate_in[k].astype(F32)
        up_pre = up_in[k].astype(F32)
        sigma = jax.nn.sigmoid(gate_pre)
        up_grad = act_grad * (gate_pre * sigma)
        gate_grad = act_grad * up_pre * sigma * (1.0 + gate_pre * (1.0 - sigma))
        ug[k] = up_grad.astype(BF)
        gg[k] = gate_grad.astype(BF)
        ug_rows[...] = jnp.transpose(ug[k])
        gg_rows[...] = jnp.transpose(gg[k])
        gate_in[k] = (gate_pre * sigma * up_pre).astype(BF)
        if k == n_wide - 1:
            saves.append(here(gg.at[k], gg_hbm, save_sem.at[0]))
            saves.append(here(ug.at[k], ug_hbm, save_sem.at[1]))
        if k == 0:
            loads[1].wait()
            loads[2].wait()
        tile = 512

        def columns(j, carry):
            at = pl.ds(pl.multiple_of(j * tile, tile), tile)
            value = jnp.dot(gg_rows[...], w_gate[:, at], preferred_element_type=F32)
            value = value + jnp.dot(ug_rows[...], w_up[:, at], preferred_element_type=F32)
            value = value.astype(BF).reshape(spots, 2, cap, tile)
            for c in range(2):
                part[k, c, :, :, at] = value[:, c]
            return carry

        lax.fori_loop(0, width // tile, columns, 0)
        halves[k] = remote(part.at[k, 1 - core], half_in.at[k], pair(half_sem, k), mz, sibling)

    returned = {}

    def give_back(k):
        halves[k].wait_recv()
        whole = part[k, core].astype(F32) + half_in[k].astype(F32)
        part[k, core] = whole.astype(BF)
        for q in range(1, spots):
            returned[k, q] = remote(
                part.at[k, core, ms ^ q], back.at[k, ms], pair(back_sem, k, q), mz, plane_id(q)
            )
        returned[k, 0] = here(part.at[k, core, ms], back.at[k, ms], keep_sem.at[k, 2])

    z_back = [None] * n_wide

    def pick(k):
        for q in range(1, spots):
            returned[k, q].wait_recv()
        returned[k, 0].wait()
        got = zdy if k else send_dy
        info = got[k, :, width:].astype(F32)
        line = lax.broadcasted_iota(jnp.int32, (rows, slots), 1)
        rank = jnp.zeros((rows, slots), F32)
        rest = line
        for e in range(spots):
            inside = (line >= e * cap) & (line < (e + 1) * cap)
            rank = jnp.where(inside, info[:, e : e + 1], rank)
            rest = jnp.where(inside, line - e * cap, rest)
        table = jnp.where(rank == rest.astype(F32), 1.0, 0.0).astype(BF)
        value = jnp.dot(table, back[k].reshape(slots, width), preferred_element_type=F32)
        pick_out[k] = value.astype(BF)
        if k:
            z_back[k] = remote(pick_out.at[k], pick_in.at[k], pair(zb_sem, k), mz ^ k, mn)

    def share_dy(k):
        share(k, 1, sd_sem)

    def share_x(k):
        share(k, 0, sx_sem)

    wide_tile = 512

    def down_tile(j, carry):
        at = pl.ds(pl.multiple_of(j * wide_tile, wide_tile), wide_tile)
        value = jnp.zeros((w_down.shape[0], wide_tile), F32)
        for k in range(n_wide):
            rows_of = dy_rows[pl.ds((mz ^ k) * n_narrow, n_narrow), :, at]
            value = value + jnp.dot(
                gate_in[k], rows_of.reshape(chunk, wide_tile), preferred_element_type=F32
            )
        w_down[:, at] = value.astype(BF)
        return carry

    def multiply_down(first, last):
        lax.fori_loop(first, last, down_tile, 0)
        if last == width // wide_tile:
            saves.append(here(w_down, down_hbm, save_sem.at[2]))

    def multiply_x(left, target):
        def tile_of(j, carry):
            at = pl.ds(pl.multiple_of(j * wide_tile, wide_tile), wide_tile)
            value = jnp.zeros((w_gate.shape[0], wide_tile), F32)
            for k in range(n_wide - 1):
                value = value + jnp.dot(
                    left[k], x_rows[k, :, :, at].reshape(chunk, wide_tile),
                    preferred_element_type=F32,
                )
            target[:, at] = value.astype(BF)
            return carry

        lax.fori_loop(0, width // wide_tile, tile_of, 0)

    def have_x(k):
        kept_x[k].wait()
        for q in range(spots):
            shared[k, q, 0].wait_recv()

    slots_dy(0)
    pack_x(0)
    pack_x(1)
    pack_dy(3)
    share_dy(0)
    slots_x(0)
    slots_dy(1)
    z_dy[2].wait_send()
    start_dy(3)
    start_x(1)
    slots_dy(2)
    pack_x(2)
    pack_x(3)
    expert(0)
    share_dy(1)
    share_x(0)
    expert(1)
    share_dy(2)
    give_back(0)
    slots_dy(3)
    z_dy[3].wait_send()
    start_x(2)
    expert(2)
    give_back(1)
    slots_x(1)
    share_dy(3)
    pick(0)
    expert(3)
    give_back(2)
    z_x[2].wait_send()
    start_x(3)
    pick(1)
    slots_x(2)
    give_back(3)
    share_x(1)
    multiply_down(0, 2)
    pick(2)
    share_x(2)
    multiply_down(2, 4)
    slots_x(3)
    for k in range(n_wide - 1):
        have_x(k)
    multiply_x(gg, w_gate)
    saves.append(here(w_gate, gate_part, save_sem.at[3]))
    pick(3)
    share_x(3)
    multiply_x(ug, w_up)
    saves.append(here(w_up, up_part, save_sem.at[4]))
    have_x(n_wide - 1)

    total = jnp.dot(spread_ref[0], pick_out[0], preferred_element_type=F32)
    for k in range(1, n_wide):
        z_back[k].wait_recv()
        total = total + jnp.dot(spread_ref[k], pick_in[k], preferred_element_type=F32)
    out_ref[...] = total.astype(BF)

    for k in range(n_wide):
        for q in range(spots):
            shared[k, q, 0].wait_send()
            shared[k, q, 1].wait_send()
            if q:
                plane[k, q, 0].wait_send()
                plane[k, q, 1].wait_send()
                returned[k, q].wait_send()
        halves[k].wait_send()
        if k:
            if k == 1:
                z_dy[k].wait_send()
            if k != 2:
                z_x[k].wait_send()
            z_back[k].wait_send()
    for copy in saves:
        copy.wait()


def exchange(tokens, out_grad, pack, spread, info, w_gate, w_up, w_down, gate_saved, up_saved):
    n_wide, n_narrow = lax.axis_size("wide"), lax.axis_size("narrow")
    devices = n_wide * n_narrow
    spots = n_narrow // 2
    count, width = tokens.shape
    rows = pack.shape[1]
    half = w_gate.shape[1]
    cap = gate_saved.shape[2] // devices
    chunk = n_narrow * cap
    wide_row = width + info.shape[2]
    flops = 6 * devices * cap * width * half
    vmem = pl.BlockSpec(memory_space=pltpu.VMEM)
    hbm = pl.BlockSpec(memory_space=pl.ANY)
    sem = pltpu.SemaphoreType.DMA
    return pl.pallas_call(
        functools.partial(exchange_kernel, n_wide, n_narrow, cap),
        out_shape=(
            jax.ShapeDtypeStruct((count, width), BF),
            jax.ShapeDtypeStruct((n_narrow, cap, width), BF),
            jax.ShapeDtypeStruct((half, width), BF),
            jax.ShapeDtypeStruct((half, width), BF),
            jax.ShapeDtypeStruct((half, width), BF),
            jax.ShapeDtypeStruct((half, chunk), BF),
            jax.ShapeDtypeStruct((half, chunk), BF),
        ),
        in_specs=[vmem] * 5 + [hbm] * 5,
        out_specs=(vmem, hbm, hbm, hbm, hbm, hbm, hbm),
        scratch_shapes=[
            pltpu.VMEM((n_wide - 1, n_narrow, cap, width), BF),
            pltpu.VMEM((n_wide, rows, width), BF),
            pltpu.VMEM((n_wide, rows, wide_row), BF),
            pltpu.VMEM((n_wide, rows, width), BF),
            pltpu.VMEM((n_wide, rows, wide_row), BF),
            pltpu.VMEM((n_wide, spots, cap, width), BF),
            pltpu.VMEM((n_wide, spots, cap, width), BF),
            pltpu.VMEM((devices, cap, width), BF),
            pltpu.VMEM((half, width), BF),
            pltpu.VMEM((half, width), BF),
            pltpu.VMEM((half, width), BF),
            pltpu.VMEM((n_wide, half, chunk), BF),
            pltpu.VMEM((n_wide, half, chunk), BF),
            pltpu.VMEM((n_wide, half, chunk), BF),
            pltpu.VMEM((n_wide, half, chunk), BF),
            pltpu.VMEM((chunk, half), BF),
            pltpu.VMEM((chunk, half), BF),
            pltpu.VMEM((n_wide, 2, spots, cap, width), BF),
            pltpu.VMEM((n_wide, spots, cap, width), BF),
            pltpu.VMEM((n_wide, spots, cap, width), BF),
            pltpu.VMEM((n_wide, rows, width), BF),
            pltpu.VMEM((n_wide, rows, width), BF),
            sem((3 + 2 * n_wide,)),
            sem((n_wide, 3)),
            sem((5,)),
            sem((2, n_wide)),
            sem((2, n_wide)),
            sem((2, n_wide, spots)),
            sem((2, n_wide, spots)),
            sem((2, n_wide, spots)),
            sem((2, n_wide, spots)),
            sem((2, n_wide)),
            sem((2, n_wide, spots)),
            sem((2, n_wide)),
        ],
        compiler_params=pltpu.CompilerParams(
            collective_id=0, has_side_effects=True, vmem_limit_bytes=VMEM_BYTES
        ),
        cost_estimate=pl.CostEstimate(flops=flops, bytes_accessed=40_000_000, transcendentals=0),
    )(tokens, out_grad, pack, spread, info, w_gate, w_up, w_down, gate_saved, up_saved)


def local_kernel(tokens, out_grad, expert_ids, gates, w_gate, w_up, w_down, gate_saved, up_saved):
    n_wide = lax.axis_size("wide")
    n_narrow = lax.axis_size("narrow")
    devices = n_wide * n_narrow
    experts = devices // 2
    spots = n_narrow // 2
    count, width = tokens.shape
    cap = gate_saved.shape[1] // devices
    rows = count * (expert_ids.shape[1] // 2) // n_wide
    picked, rank, gate = route_tables(expert_ids, gates, experts, cap)
    groups = lax.axis_index("wide") ^ jnp.arange(n_wide, dtype=jnp.int32)
    member = jnp.any(picked.reshape(count, n_wide, spots), axis=2)
    row = lax.broadcasted_iota(jnp.int32, (count, count), 0)
    col = lax.broadcasted_iota(jnp.int32, (count, count), 1)
    place = jnp.dot((col < row).astype(BF), member.astype(BF), preferred_element_type=F32)
    place = jnp.take(jnp.where(member, place, -1.0), groups, axis=1).T
    number = jnp.arange(rows, dtype=F32)
    spread = (place[:, :, None] == number[None, None, :]).astype(BF)
    pack = (place[:, None, :] == number[None, :, None]).astype(BF)
    info = jnp.concatenate([rank.reshape(count, n_wide, spots), gate.reshape(count, n_wide, spots)], 2)
    info = jnp.take(info, groups, axis=1).astype(BF).transpose(1, 0, 2)
    info = jnp.pad(info, ((0, 0), (0, 0), (0, 128 - 2 * spots)))
    info = jnp.einsum("krt,ktc->krc", pack, info, preferred_element_type=F32).astype(BF)
    turned_gate, turned_up = gate_saved.swapaxes(1, 2), up_saved.swapaxes(1, 2)
    token_grad, rows_x, grad_down, gate_part, up_part, gate_grad, up_grad = exchange(
        tokens, out_grad, pack, spread, info, w_gate.swapaxes(1, 2), w_up.swapaxes(1, 2), w_down,
        gate_saved.swapaxes(1, 2), up_saved.swapaxes(1, 2),
    )
    rows_x = rows_x.reshape(n_narrow * cap, width)
    grad_gate = jnp.dot(gate_grad, rows_x, preferred_element_type=F32) + gate_part.astype(F32)
    grad_up = jnp.dot(up_grad, rows_x, preferred_element_type=F32) + up_part.astype(F32)
    return (token_grad, grad_gate.astype(BF).T[None], grad_up.astype(BF).T[None], grad_down[None])


def local(tokens, out_grad, expert_ids, gates, w_gate, w_up, w_down, gate_saved, up_saved):
    slots = gate_saved.shape[1]
    cap = slots // (lax.axis_size("wide") * lax.axis_size("narrow"))
    fits = 8 * slots * tokens.shape[1] <= VMEM_BYTES and cap % 16 == 0
    fits = fits and lax.axis_size("wide") == 4
    body = local_kernel if fits else local_permutes
    return body(tokens, out_grad, expert_ids, gates, w_gate, w_up, w_down, gate_saved, up_saved)


def solution(mesh):
    row = P(("wide", "narrow"), None)
    slab = P(("wide", "narrow"), None, None)
    return jax.shard_map(
        local,
        mesh=mesh,
        in_specs=(row, row, row, row, slab, slab, slab, slab, slab),
        out_specs=(row, slab, slab, slab),
        check_vma=False,
    )
```

```python
import functools

import jax
import jax.numpy as jnp
from jax import lax
from jax.experimental import pallas as pl
from jax.experimental.pallas import tpu as pltpu
from jax.sharding import PartitionSpec as P

BF = jnp.bfloat16
F32 = jnp.float32
ACROSS = (((0,), (0,)), ((), ()))
INNER = (((1,), (1,)), ((), ()))
MESH = pl.DeviceIdType.MESH
VMEM_BYTES = 63 * 1024 * 1024


def swap(value, axis, shift):
    if shift == 0:
        return value
    size = lax.axis_size(axis)
    return lax.ppermute(value, axis, [(i, i ^ shift) for i in range(size)])


def route_tables(ids, gates, experts, cap):
    count = ids.shape[0]
    hit = ids[:, :, None] == jnp.arange(experts, dtype=jnp.int32)[None, None, :]
    picked = jnp.any(hit, axis=1)
    gate = jnp.sum(jnp.where(hit, gates.astype(F32)[:, :, None], 0.0), axis=1)
    row = lax.broadcasted_iota(jnp.int32, (count, count), 0)
    col = lax.broadcasted_iota(jnp.int32, (count, count), 1)
    rank = jnp.dot((col < row).astype(BF), picked.astype(BF), preferred_element_type=F32)
    rank = jnp.where(picked & (rank < cap), rank, -1.0)
    return picked, rank, gate


def local_permutes(tokens, out_grad, expert_ids, gates, w_gate, w_up, w_down, gate_saved, up_saved):
    n_wide = lax.axis_size("wide")
    n_narrow = lax.axis_size("narrow")
    devices = n_wide * n_narrow
    experts = devices // 2
    spots = n_narrow // 2
    count, width = tokens.shape
    half = w_gate.shape[2]
    cap = gate_saved.shape[1] // devices
    rows = count * (expert_ids.shape[1] // 2) // n_wide
    my_wide = lax.axis_index("wide")
    my_narrow = lax.axis_index("narrow")
    my_spot = my_narrow // 2
    me = my_wide * n_narrow + my_narrow

    picked, rank, gate = route_tables(expert_ids, gates, experts, cap)
    groups = my_wide ^ jnp.arange(n_wide, dtype=jnp.int32)
    member = jnp.any(picked.reshape(count, n_wide, spots), axis=2)
    row = lax.broadcasted_iota(jnp.int32, (count, count), 0)
    col = lax.broadcasted_iota(jnp.int32, (count, count), 1)
    place = jnp.dot((col < row).astype(BF), member.astype(BF), preferred_element_type=F32)
    place = jnp.where(member, place, -1.0)
    place = jnp.take(place, groups, axis=1)
    pack = (place[:, :, None] == jnp.arange(rows, dtype=F32)[None, None, :]).astype(BF)
    pack = pack.reshape(count, n_wide * rows)
    info = jnp.concatenate([rank.reshape(count, n_wide, spots), gate.reshape(count, n_wide, spots)], 2)
    info = jnp.take(info, groups, axis=1).astype(BF)

    order = me ^ jnp.arange(devices, dtype=jnp.int32)
    gate_rows = jnp.take(gate_saved[0].reshape(devices, cap, half), order, axis=0)
    up_rows = jnp.take(up_saved[0].reshape(devices, cap, half), order, axis=0)
    gate_rows = gate_rows.reshape(n_wide, n_narrow * cap, half)
    up_rows = up_rows.reshape(n_wide, n_narrow * cap, half)

    spot_order = my_spot ^ jnp.arange(spots, dtype=jnp.int32)
    weight_gate, weight_up, weight_down = w_gate[0], w_up[0], w_down[0]

    arrived = []
    for step in range(n_wide):
        mine = pack[:, step * rows : (step + 1) * rows]
        sent_x = lax.dot_general(mine, tokens, ACROSS, preferred_element_type=F32).astype(BF)
        sent_dy = lax.dot_general(mine, out_grad, ACROSS, preferred_element_type=F32).astype(BF)
        sent_info = lax.dot_general(mine, info[:, step], ACROSS, preferred_element_type=F32).astype(BF)
        sent_info = jnp.pad(sent_info, ((0, 0), (0, 128 - 2 * spots)))
        sent = jnp.concatenate([sent_x, sent_dy, sent_info], axis=1)
        arrived.append(swap(sent, "wide", step))

    tables, all_x, all_dy, all_act, all_gate, all_up, partials = [], [], [], [], [], [], []
    for step in range(n_wide):
        got = arrived[step]
        got_rank = jnp.take(got[:, 2 * width : 2 * width + spots], spot_order, axis=1).astype(F32)
        got_gate = jnp.take(got[:, 2 * width + spots : 2 * width + 2 * spots], spot_order, axis=1)
        hits = got_rank[:, :, None] == jnp.arange(cap, dtype=F32)[None, None, :]
        table = hits.astype(BF).reshape(rows, spots * cap)
        scaled = jnp.where(hits, got_gate[:, :, None], jnp.zeros((), BF)).reshape(rows, spots * cap)
        tables.append(table)
        x_slot = lax.dot_general(table, got[:, :width], ACROSS, preferred_element_type=F32).astype(BF)
        dy_slot = lax.dot_general(
            scaled, got[:, width : 2 * width], ACROSS, preferred_element_type=F32
        ).astype(BF)
        both = jnp.stack([x_slot.reshape(spots, cap, width), dy_slot.reshape(spots, cap, width)], 1)
        plane = jnp.stack([swap(both[k], "narrow", 2 * k) for k in range(spots)])
        chip = jnp.stack([plane, swap(plane, "narrow", 1)], 1)
        rows_x = chip[:, :, 0].reshape(n_narrow * cap, width)
        rows_dy = chip[:, :, 1].reshape(n_narrow * cap, width)
        gate_pre = gate_rows[step].astype(F32)
        up_pre = up_rows[step].astype(F32)
        sigma = jax.nn.sigmoid(gate_pre)
        silu = gate_pre * sigma
        act = (silu * up_pre).astype(BF)
        act_grad = lax.dot_general(rows_dy, weight_down, INNER, preferred_element_type=F32)
        up_grad = (act_grad * silu).astype(BF)
        gate_grad = (act_grad * up_pre * sigma * (1.0 + gate_pre * (1.0 - sigma))).astype(BF)
        partial = lax.dot_general(gate_grad, weight_gate, INNER, preferred_element_type=F32)
        partial = partial + lax.dot_general(up_grad, weight_up, INNER, preferred_element_type=F32)
        all_x.append(rows_x)
        all_dy.append(rows_dy)
        all_act.append(act)
        all_gate.append(gate_grad)
        all_up.append(up_grad)
        partials.append(partial.astype(BF).reshape(spots, 2, cap, width))

    token_grad = jnp.zeros((count, width), F32)
    for step in range(n_wide):
        partial = partials[step]
        whole = partial[:, 0].astype(F32) + swap(partial[:, 1], "narrow", 1).astype(F32)
        whole = whole.astype(BF)
        back = jnp.concatenate([swap(whole[k], "narrow", 2 * k) for k in range(spots)], 0)
        part = jnp.dot(tables[step], back, preferred_element_type=F32).astype(BF)
        part = swap(part, "wide", step)
        token_grad = token_grad + jnp.dot(
            pack[:, step * rows : (step + 1) * rows], part, preferred_element_type=F32
        )

    cat_x = jnp.concatenate(all_x, 0)
    cat_dy = jnp.concatenate(all_dy, 0)
    cat_act = jnp.concatenate(all_act, 0)
    cat_gate = jnp.concatenate(all_gate, 0)
    cat_up = jnp.concatenate(all_up, 0)
    grad_gate = lax.dot_general(cat_x, cat_gate, ACROSS, preferred_element_type=F32).astype(BF)
    grad_up = lax.dot_general(cat_x, cat_up, ACROSS, preferred_element_type=F32).astype(BF)
    grad_down = lax.dot_general(cat_act, cat_dy, ACROSS, preferred_element_type=F32).astype(BF)
    return (token_grad.astype(BF), grad_gate[None], grad_up[None], grad_down[None])


def exchange_kernel(
    n_wide, n_narrow, cap, tokens_ref, grad_ref, pack_ref, spread_ref, info_ref, wg_hbm, wu_hbm,
    wd_hbm, gate_hbm, up_hbm, out_ref, x_last, down_hbm, gate_part,
    up_part, gg_hbm, ug_hbm, x_rows, send_x, send_dy, zx, zdy,
    stage_x, stage_dy, dy_rows, w_gate, w_up, w_down, gate_in, up_in, gg, ug, gg_rows, ug_rows, part, half_in, back, pick_out, pick_in,
    load_sem, keep_sem, save_sem, zx_sem, zdy_sem, px_sem, pd_sem, sx_sem, sd_sem, half_sem, back_sem, zb_sem,
):
    spots = n_narrow // 2
    width = tokens_ref.shape[1]
    rows = pack_ref.shape[1]
    slots = spots * cap
    chunk = n_narrow * cap
    mz = lax.axis_index("wide")
    mn = lax.axis_index("narrow")
    ms = mn // 2
    core = mn - 2 * ms
    sibling = ms * 2 + (1 - core)

    def plane_id(q):
        return (ms ^ q) * 2 + core

    def remote(src, dst, sems, wide, narrow):
        copy = pltpu.make_async_remote_copy(
            src_ref=src, dst_ref=dst, send_sem=sems[0], recv_sem=sems[1],
            device_id=(wide, narrow), device_id_type=MESH,
        )
        copy.start()
        return copy

    def pair(sem, *index):
        return sem.at[(0, *index)], sem.at[(1, *index)]

    def here(src, dst, sem):
        copy = pltpu.make_async_copy(src, dst, sem)
        copy.start()
        return copy

    loads = [
        here(wd_hbm.at[0], w_down, load_sem.at[0]),
        here(wg_hbm.at[0], w_gate, load_sem.at[1]),
        here(wu_hbm.at[0], w_up, load_sem.at[2]),
    ]
    saved = []
    for k in range(n_wide):
        source = pl.ds(pl.multiple_of((mz ^ k) * chunk, 128), chunk)
        saved.append((
            here(gate_hbm.at[0, :, source], gate_in.at[k], load_sem.at[3 + 2 * k]),
            here(up_hbm.at[0, :, source], up_in.at[k], load_sem.at[4 + 2 * k]),
        ))

    barrier = pltpu.get_barrier_semaphore()
    for k in range(1, n_wide):
        pl.semaphore_signal(barrier, inc=1, device_id=(mz ^ k, mn), device_id_type=MESH)
    for q in range(1, spots):
        pl.semaphore_signal(barrier, inc=1, device_id=(mz, plane_id(q)), device_id_type=MESH)
    pl.semaphore_signal(barrier, inc=1, device_id=(mz, sibling), device_id_type=MESH)

    def pack_dy(k):
        send_dy[k, :, :width] = jnp.dot(
            pack_ref[k], grad_ref[...], preferred_element_type=F32
        ).astype(BF)
        send_dy[k, :, width:] = info_ref[k]

    def pack_x(k):
        send_x[k] = jnp.dot(pack_ref[k], tokens_ref[...], preferred_element_type=F32).astype(BF)

    z_dy, z_x = [None] * n_wide, [None] * n_wide

    def start_dy(k):
        z_dy[k] = remote(send_dy.at[k], zdy.at[k], pair(zdy_sem, k), mz ^ k, mn)

    def start_x(k):
        z_x[k] = remote(send_x.at[k], zx.at[k], pair(zx_sem, k), mz ^ k, mn)

    pack_dy(2)
    pl.semaphore_wait(barrier, n_wide - 1 + spots - 1 + 1)
    start_dy(2)
    pack_dy(1)
    start_dy(1)
    pack_dy(0)

    kept_dy, kept_x = {}, {}
    plane, shared = {}, {}

    def tables(k):
        got = zdy if k else send_dy
        info = jnp.transpose(got[k, :, width:].astype(F32))
        line = lax.broadcasted_iota(jnp.int32, (slots, rows), 0)
        rank = jnp.zeros((slots, rows), F32)
        gate = jnp.zeros((slots, rows), F32)
        rest = line
        for e in range(spots):
            inside = (line >= e * cap) & (line < (e + 1) * cap)
            rank = jnp.where(inside, info[e : e + 1, :], rank)
            gate = jnp.where(inside, info[spots + e : spots + e + 1, :], gate)
            rest = jnp.where(inside, line - e * cap, rest)
        return rank == rest.astype(F32), gate

    def slots_dy(k):
        if k:
            z_dy[k].wait_recv()
        got = zdy if k else send_dy
        hit, gate = tables(k)
        scaled = jnp.where(hit, gate, 0.0).astype(BF)
        stage_dy[k] = jnp.dot(scaled, got[k, :, :width], preferred_element_type=F32).astype(
            BF
        ).reshape(spots, cap, width)
        to = (mz ^ k) * n_narrow + mn
        for q in range(1, spots):
            plane[k, q, 1] = remote(
                stage_dy.at[k, ms ^ q], dy_rows.at[to], pair(pd_sem, k, q), mz, plane_id(q)
            )
        kept_dy[k] = here(stage_dy.at[k, ms], dy_rows.at[to], keep_sem.at[k, 0])
        shared[k, 0, 1] = remote(
            stage_dy.at[k, ms], dy_rows.at[to], pair(sd_sem, k, 0), mz, sibling
        )

    def x_at(k, n):
        return x_last.at[n] if k == n_wide - 1 else x_rows.at[k, n]

    def slots_x(k):
        if k:
            z_x[k].wait_recv()
        got = zx if k else send_x
        table = jnp.where(tables(k)[0], 1.0, 0.0).astype(BF)
        stage_x[k] = jnp.dot(table, got[k], preferred_element_type=F32).astype(BF).reshape(
            spots, cap, width
        )
        to = x_at(k, mn)
        for q in range(1, spots):
            plane[k, q, 0] = remote(
                stage_x.at[k, ms ^ q], to, pair(px_sem, k, q), mz, plane_id(q)
            )
        kept_x[k] = here(stage_x.at[k, ms], to, keep_sem.at[k, 1])
        shared[k, 0, 0] = remote(stage_x.at[k, ms], to, pair(sx_sem, k, 0), mz, sibling)

    def share(k, which, sem):
        for q in range(1, spots):
            plane[k, q, which].wait_recv()
            if which:
                at = dy_rows.at[(mz ^ k) * n_narrow + plane_id(q)]
            else:
                at = x_at(k, plane_id(q))
            shared[k, q, which] = remote(at, at, pair(sem, k, q), mz, sibling)

    halves = [None] * n_wide
    saves = []

    def expert(k):
        kept_dy[k].wait()
        for q in range(spots):
            shared[k, q, 1].wait_recv()
        if k == 0:
            loads[0].wait()
        for copy in saved[k]:
            copy.wait()
        source = pl.ds((mz ^ k) * n_narrow, n_narrow)
        dy = dy_rows[source].reshape(chunk, width)
        act_grad = lax.dot_general(w_down[...], dy, INNER, preferred_element_type=F32)
        gate_pre = gate_in[k].astype(F32)
        up_pre = up_in[k].astype(F32)
        sigma = jax.nn.sigmoid(gate_pre)
        up_grad = act_grad * (gate_pre * sigma)
        gate_grad = act_grad * up_pre * sigma * (1.0 + gate_pre * (1.0 - sigma))
        ug[k] = up_grad.astype(BF)
        gg[k] = gate_grad.astype(BF)
        ug_rows[...] = jnp.transpose(ug[k])
        gg_rows[...] = jnp.transpose(gg[k])
        gate_in[k] = (gate_pre * sigma * up_pre).astype(BF)
        if k == n_wide - 1:
            saves.append(here(gg.at[k], gg_hbm, save_sem.at[0]))
            saves.append(here(ug.at[k], ug_hbm, save_sem.at[1]))
        if k == 0:
            loads[1].wait()
            loads[2].wait()
        tile = 512

        def columns(j, carry):
            at = pl.ds(pl.multiple_of(j * tile, tile), tile)
            value = jnp.dot(gg_rows[...], w_gate[:, at], preferred_element_type=F32)
            value = value + jnp.dot(ug_rows[...], w_up[:, at], preferred_element_type=F32)
            value = value.astype(BF).reshape(spots, 2, cap, tile)
            for c in range(2):
                part[k, c, :, :, at] = value[:, c]
            return carry

        lax.fori_loop(0, width // tile, columns, 0)
        halves[k] = remote(part.at[k, 1 - core], half_in.at[k], pair(half_sem, k), mz, sibling)

    returned = {}

    def give_back(k):
        halves[k].wait_recv()
        whole = part[k, core].astype(F32) + half_in[k].astype(F32)
        part[k, core] = whole.astype(BF)
        for q in range(1, spots):
            returned[k, q] = remote(
                part.at[k, core, ms ^ q], back.at[k, ms], pair(back_sem, k, q), mz, plane_id(q)
            )
        returned[k, 0] = here(part.at[k, core, ms], back.at[k, ms], keep_sem.at[k, 2])

    z_back = [None] * n_wide

    def pick(k):
        for q in range(1, spots):
            returned[k, q].wait_recv()
        returned[k, 0].wait()
        got = zdy if k else send_dy
        info = got[k, :, width:].astype(F32)
        line = lax.broadcasted_iota(jnp.int32, (rows, slots), 1)
        rank = jnp.zeros((rows, slots), F32)
        rest = line
        for e in range(spots):
            inside = (line >= e * cap) & (line < (e + 1) * cap)
            rank = jnp.where(inside, info[:, e : e + 1], rank)
            rest = jnp.where(inside, line - e * cap, rest)
        table = jnp.where(rank == rest.astype(F32), 1.0, 0.0).astype(BF)
        value = jnp.dot(table, back[k].reshape(slots, width), preferred_element_type=F32)
        pick_out[k] = value.astype(BF)
        if k:
            z_back[k] = remote(pick_out.at[k], pick_in.at[k], pair(zb_sem, k), mz ^ k, mn)

    def share_dy(k):
        share(k, 1, sd_sem)

    def share_x(k):
        share(k, 0, sx_sem)

    wide_tile = 512

    def down_tile(j, carry):
        at = pl.ds(pl.multiple_of(j * wide_tile, wide_tile), wide_tile)
        value = jnp.zeros((w_down.shape[0], wide_tile), F32)
        for k in range(n_wide):
            rows_of = dy_rows[pl.ds((mz ^ k) * n_narrow, n_narrow), :, at]
            value = value + jnp.dot(
                gate_in[k], rows_of.reshape(chunk, wide_tile), preferred_element_type=F32
            )
        w_down[:, at] = value.astype(BF)
        return carry

    def multiply_down(first, last):
        lax.fori_loop(first, last, down_tile, 0)
        if last == width // wide_tile:
            saves.append(here(w_down, down_hbm, save_sem.at[2]))

    def multiply_x(left, target):
        def tile_of(j, carry):
            at = pl.ds(pl.multiple_of(j * wide_tile, wide_tile), wide_tile)
            value = jnp.zeros((w_gate.shape[0], wide_tile), F32)
            for k in range(n_wide - 1):
                value = value + jnp.dot(
                    left[k], x_rows[k, :, :, at].reshape(chunk, wide_tile),
                    preferred_element_type=F32,
                )
            target[:, at] = value.astype(BF)
            return carry

        lax.fori_loop(0, width // wide_tile, tile_of, 0)

    def have_x(k):
        kept_x[k].wait()
        for q in range(spots):
            shared[k, q, 0].wait_recv()

    slots_dy(0)
    pack_x(0)
    pack_x(1)
    pack_dy(3)
    share_dy(0)
    slots_x(0)
    slots_dy(1)
    z_dy[2].wait_send()
    start_dy(3)
    start_x(1)
    slots_dy(2)
    pack_x(2)
    pack_x(3)
    expert(0)
    share_dy(1)
    share_x(0)
    expert(1)
    share_dy(2)
    give_back(0)
    slots_dy(3)
    z_dy[3].wait_send()
    start_x(2)
    expert(2)
    give_back(1)
    start_x(3)
    slots_x(1)
    share_dy(3)
    pick(0)
    expert(3)
    give_back(2)
    pick(1)
    slots_x(2)
    give_back(3)
    share_x(1)
    multiply_down(0, 2)
    pick(2)
    share_x(2)
    multiply_down(2, 4)
    slots_x(3)
    for k in range(n_wide - 1):
        have_x(k)
    multiply_x(gg, w_gate)
    saves.append(here(w_gate, gate_part, save_sem.at[3]))
    pick(3)
    share_x(3)
    multiply_x(ug, w_up)
    saves.append(here(w_up, up_part, save_sem.at[4]))
    have_x(n_wide - 1)

    total = jnp.dot(spread_ref[0], pick_out[0], preferred_element_type=F32)
    for k in range(1, n_wide):
        z_back[k].wait_recv()
        total = total + jnp.dot(spread_ref[k], pick_in[k], preferred_element_type=F32)
    out_ref[...] = total.astype(BF)

    for k in range(n_wide):
        for q in range(spots):
            shared[k, q, 0].wait_send()
            shared[k, q, 1].wait_send()
            if q:
                plane[k, q, 0].wait_send()
                plane[k, q, 1].wait_send()
                returned[k, q].wait_send()
        halves[k].wait_send()
        if k:
            if k == 1:
                z_dy[k].wait_send()
            z_x[k].wait_send()
            z_back[k].wait_send()
    for copy in saves:
        copy.wait()


def exchange(tokens, out_grad, pack, spread, info, w_gate, w_up, w_down, gate_saved, up_saved):
    n_wide, n_narrow = lax.axis_size("wide"), lax.axis_size("narrow")
    devices = n_wide * n_narrow
    spots = n_narrow // 2
    count, width = tokens.shape
    rows = pack.shape[1]
    half = w_gate.shape[1]
    cap = gate_saved.shape[2] // devices
    chunk = n_narrow * cap
    wide_row = width + info.shape[2]
    flops = 6 * devices * cap * width * half
    vmem = pl.BlockSpec(memory_space=pltpu.VMEM)
    hbm = pl.BlockSpec(memory_space=pl.ANY)
    sem = pltpu.SemaphoreType.DMA
    return pl.pallas_call(
        functools.partial(exchange_kernel, n_wide, n_narrow, cap),
        out_shape=(
            jax.ShapeDtypeStruct((count, width), BF),
            jax.ShapeDtypeStruct((n_narrow, cap, width), BF),
            jax.ShapeDtypeStruct((half, width), BF),
            jax.ShapeDtypeStruct((half, width), BF),
            jax.ShapeDtypeStruct((half, width), BF),
            jax.ShapeDtypeStruct((half, chunk), BF),
            jax.ShapeDtypeStruct((half, chunk), BF),
        ),
        in_specs=[vmem] * 5 + [hbm] * 5,
        out_specs=(vmem, hbm, hbm, hbm, hbm, hbm, hbm),
        scratch_shapes=[
            pltpu.VMEM((n_wide - 1, n_narrow, cap, width), BF),
            pltpu.VMEM((n_wide, rows, width), BF),
            pltpu.VMEM((n_wide, rows, wide_row), BF),
            pltpu.VMEM((n_wide, rows, width), BF),
            pltpu.VMEM((n_wide, rows, wide_row), BF),
            pltpu.VMEM((n_wide, spots, cap, width), BF),
            pltpu.VMEM((n_wide, spots, cap, width), BF),
            pltpu.VMEM((devices, cap, width), BF),
            pltpu.VMEM((half, width), BF),
            pltpu.VMEM((half, width), BF),
            pltpu.VMEM((half, width), BF),
            pltpu.VMEM((n_wide, half, chunk), BF),
            pltpu.VMEM((n_wide, half, chunk), BF),
            pltpu.VMEM((n_wide, half, chunk), BF),
            pltpu.VMEM((n_wide, half, chunk), BF),
            pltpu.VMEM((chunk, half), BF),
            pltpu.VMEM((chunk, half), BF),
            pltpu.VMEM((n_wide, 2, spots, cap, width), BF),
            pltpu.VMEM((n_wide, spots, cap, width), BF),
            pltpu.VMEM((n_wide, spots, cap, width), BF),
            pltpu.VMEM((n_wide, rows, width), BF),
            pltpu.VMEM((n_wide, rows, width), BF),
            sem((3 + 2 * n_wide,)),
            sem((n_wide, 3)),
            sem((5,)),
            sem((2, n_wide)),
            sem((2, n_wide)),
            sem((2, n_wide, spots)),
            sem((2, n_wide, spots)),
            sem((2, n_wide, spots)),
            sem((2, n_wide, spots)),
            sem((2, n_wide)),
            sem((2, n_wide, spots)),
            sem((2, n_wide)),
        ],
        compiler_params=pltpu.CompilerParams(
            collective_id=0, has_side_effects=True, vmem_limit_bytes=VMEM_BYTES
        ),
        cost_estimate=pl.CostEstimate(flops=flops, bytes_accessed=40_000_000, transcendentals=0),
    )(tokens, out_grad, pack, spread, info, w_gate, w_up, w_down, gate_saved, up_saved)


def local_kernel(tokens, out_grad, expert_ids, gates, w_gate, w_up, w_down, gate_saved, up_saved):
    n_wide = lax.axis_size("wide")
    n_narrow = lax.axis_size("narrow")
    devices = n_wide * n_narrow
    experts = devices // 2
    spots = n_narrow // 2
    count, width = tokens.shape
    cap = gate_saved.shape[1] // devices
    rows = count * (expert_ids.shape[1] // 2) // n_wide
    picked, rank, gate = route_tables(expert_ids, gates, experts, cap)
    groups = lax.axis_index("wide") ^ jnp.arange(n_wide, dtype=jnp.int32)
    member = jnp.any(picked.reshape(count, n_wide, spots), axis=2)
    row = lax.broadcasted_iota(jnp.int32, (count, count), 0)
    col = lax.broadcasted_iota(jnp.int32, (count, count), 1)
    place = jnp.dot((col < row).astype(BF), member.astype(BF), preferred_element_type=F32)
    place = jnp.take(jnp.where(member, place, -1.0), groups, axis=1).T
    number = jnp.arange(rows, dtype=F32)
    spread = (place[:, :, None] == number[None, None, :]).astype(BF)
    pack = (place[:, None, :] == number[None, :, None]).astype(BF)
    info = jnp.concatenate([rank.reshape(count, n_wide, spots), gate.reshape(count, n_wide, spots)], 2)
    info = jnp.take(info, groups, axis=1).astype(BF).transpose(1, 0, 2)
    info = jnp.pad(info, ((0, 0), (0, 0), (0, 128 - 2 * spots)))
    info = jnp.einsum("krt,ktc->krc", pack, info, preferred_element_type=F32).astype(BF)
    turned_gate, turned_up = gate_saved.swapaxes(1, 2), up_saved.swapaxes(1, 2)
    token_grad, rows_x, grad_down, gate_part, up_part, gate_grad, up_grad = exchange(
        tokens, out_grad, pack, spread, info, w_gate.swapaxes(1, 2), w_up.swapaxes(1, 2), w_down,
        gate_saved.swapaxes(1, 2), up_saved.swapaxes(1, 2),
    )
    rows_x = rows_x.reshape(n_narrow * cap, width)
    grad_gate = jnp.dot(gate_grad, rows_x, preferred_element_type=F32) + gate_part.astype(F32)
    grad_up = jnp.dot(up_grad, rows_x, preferred_element_type=F32) + up_part.astype(F32)
    return (token_grad, grad_gate.astype(BF).T[None], grad_up.astype(BF).T[None], grad_down[None])


def local(tokens, out_grad, expert_ids, gates, w_gate, w_up, w_down, gate_saved, up_saved):
    slots = gate_saved.shape[1]
    cap = slots // (lax.axis_size("wide") * lax.axis_size("narrow"))
    fits = 8 * slots * tokens.shape[1] <= VMEM_BYTES and cap % 16 == 0
    fits = fits and lax.axis_size("wide") == 4
    body = local_kernel if fits else local_permutes
    return body(tokens, out_grad, expert_ids, gates, w_gate, w_up, w_down, gate_saved, up_saved)


def solution(mesh):
    row = P(("wide", "narrow"), None)
    slab = P(("wide", "narrow"), None, None)
    return jax.shard_map(
        local,
        mesh=mesh,
        in_specs=(row, row, row, row, slab, slab, slab, slab, slab),
        out_specs=(row, slab, slab, slab),
        check_vma=False,
    )
```
